256 devices in a mesh: dp: 8 (over x, y_hi), pencil: 32 (over z, y_lo, core).
Axes of the slice: x: 4, y: 4 (y_hi: 2, y_lo: 2; y = y_hi * 2 + y_lo), z: 8, core: 2. Of those that a mesh axis runs over, the one named last changes fastest.
Arguments:
- fields: bfloat16 [8, 256, 32, 4096], P('dp', 'pencil'), may hold values from -6 to 6
- cotangent: bfloat16 [8, 256, 32, 4096], P('dp', 'pencil'), may hold values from -6 to 6
- spectral_weight: bfloat16 [32, 2, 512, 1024], P(None, None, 'pencil'), may hold values from -4 to 4
Outputs:
- grad_fields: bfloat16 [8, 256, 32, 4096], P('dp', 'pencil')
- grad_weight: float32 [32, 2, 512, 1024], P('dp', None, 'pencil')
The draws below stay inside these ranges and needn't reach their ends.
All inputs are finite; a program needn't handle non-finite values.
Results may differ from the reference program's by a relative error of at most 0.023.
Values may be sent and summed in bfloat16 or wider, within the bound.
A program may use at most 128 MiB of HBM per device.

```python
import jax
import jax.numpy as jnp
from jax import lax

C = 32
MX = 32
MY = 32
MZ = 16
NY = 128
NZ = 32
NX = 256
GROUPS = 8
MP = 512
PLANE = 4096


def levels(rng, dims, shards, smallest, top_value):
    factor_of = 1.0
    for position, shards_of in shards:
        draws = jax.random.uniform(jax.random.fold_in(jax.random.fold_in(rng, 6), position), (shards_of,), jnp.float32, smallest / len(shards), top_value / len(shards))
        factor_of = factor_of * jnp.repeat(jnp.exp(draws), dims[position] // shards_of).reshape((-1,) + (1,) * (len(dims) - 1 - position))
    return factor_of


def gaussian(own_key, extent, deviation, reach, cuts=(), held_as=jnp.bfloat16):
    factor_of = levels(own_key, extent, cuts, -0.22, 0.18) if cuts else 1.0
    entries = jax.random.normal(own_key, extent, jnp.float32) * deviation * factor_of
    return jnp.minimum(jnp.maximum(entries, -reach), reach).astype(held_as)


def setup_inputs(seed: int = 0) -> dict:
    streams_of = jax.random.split(jax.random.key(seed), 4)
    return {
        "fields": gaussian(streams_of[0], (GROUPS, NX, C, PLANE), 1.0, 6.0, ((0, 8), (1, 32))),
        "cotangent": gaussian(streams_of[1], (GROUPS, NX, C, PLANE), 1.0, 6.0, ((0, 8), (1, 32))),
        "spectral_weight": gaussian(streams_of[2], (MX, 2, MP, C * C), ((NX * NY * NZ / (4 * MX * MY * MZ * C)) ** 0.5), 4.0, ((2, 32),)),
    }


root_half = 0.7071067811865476
normal_density = 0.3989422804014327


def kept_modes(count, length):
    return jnp.mod(jnp.arange(count, dtype=jnp.int32) - count // 2, length).astype(jnp.int32)


def rounded(values):
    narrow = lax.optimization_barrier(values.astype(jnp.bfloat16))
    return narrow.astype(jnp.float32)


def gelu_slope(values):
    return 0.5 * (1.0 + lax.erf(values * root_half)) + values * jnp.exp(-0.5 * values * values) * normal_density


def plane_forward(planes):
    rows = planes.shape[0]
    depth = jnp.fft.fft(planes, axis=3)[..., :MZ]
    cross = jnp.take(jnp.fft.fft(depth, axis=2), kept_modes(MY, NY), axis=2)
    return jnp.stack([cross.real, cross.imag], axis=2).reshape(rows, C, 2, MY * MZ)


def first_forward(plane_spec):
    joined = lax.complex(plane_spec[:, :, 0], plane_spec[:, :, 1])
    spectrum = jnp.take(jnp.fft.fft(joined, axis=0), kept_modes(MX, NX), axis=0)
    return jnp.transpose(jnp.stack([spectrum.real, spectrum.imag], axis=1), (0, 1, 3, 2))


def first_inverse(modes_in):
    joined = lax.complex(modes_in[:, 0], modes_in[:, 1])
    padded = jnp.zeros((NX,) + joined.shape[1:], joined.dtype).at[kept_modes(MX, NX)].set(joined)
    signal = jnp.fft.ifft(padded, axis=0) * NX
    return jnp.transpose(jnp.stack([signal.real, signal.imag], axis=2), (0, 3, 2, 1))


def plane_inverse(plane_spec, depth_weight):
    rows = plane_spec.shape[0]
    joined = lax.complex(plane_spec[:, :, 0], plane_spec[:, :, 1]).reshape(rows, C, MY, MZ)
    padded = jnp.zeros((rows, C, NY, MZ), joined.dtype).at[:, :, kept_modes(MY, NY)].set(joined)
    cross = jnp.fft.ifft(padded, axis=2) * NY * depth_weight
    deeper = jnp.zeros((rows, C, NY, NZ), joined.dtype).at[:, :, :, :MZ].set(cross)
    grid = jnp.fft.ifft(deeper, axis=3).real * NZ
    return jnp.transpose(grid, (0, 1, 3, 2)).reshape(rows, C, NZ * NY)


def to_grid(flat):
    return jnp.transpose(flat.reshape(NX, C, NZ, NY), (0, 1, 3, 2))


def forward_mix(left, right):
    return jnp.einsum('ami,amio->amo', left, right, precision=lax.Precision.HIGHEST)


def backward_mix(left, right):
    return jnp.einsum('amo,amio->ami', left, right, precision=lax.Precision.HIGHEST)


def outer_terms(left, right):
    return jnp.einsum('ami,amo->amio', left, right, precision=lax.Precision.HIGHEST)


def reference(fields, cotangent, spectral_weight):
    pairs = MY * MZ
    weight = spectral_weight.astype(jnp.float32).reshape(MX, 2, pairs, C, C)
    real_w, imag_w = weight[:, 0], weight[:, 1]
    volume = float(NX * NY * NZ)
    depth_weight = jnp.where(jnp.arange(MZ) == 0, 1.0, 2.0).astype(jnp.float32)
    mode_scale = jnp.tile(depth_weight, MY) / volume
    plain_weight = jnp.ones((MZ,), jnp.float32)

    def one_sample(carry, inputs):
        sample, grad_out = inputs
        planes = to_grid(sample.astype(jnp.float32))
        plane_spec = rounded(plane_forward(planes))
        spec_in = rounded(first_forward(plane_spec))
        real_in, imag_in = spec_in[:, 0], spec_in[:, 1]
        real_out = forward_mix(real_in, real_w) - forward_mix(imag_in, imag_w)
        imag_out = forward_mix(real_in, imag_w) + forward_mix(imag_in, real_w)
        spec_out = rounded(jnp.stack([real_out, imag_out], axis=1))
        back_x = rounded(first_inverse(spec_out))
        pre = plane_inverse(back_x, depth_weight) / volume
        grad_pre = rounded(grad_out.astype(jnp.float32) * gelu_slope(pre))
        grad_plane = rounded(plane_forward(to_grid(grad_pre)))
        grad_spec = rounded(first_forward(grad_plane) * mode_scale[None, None, :, None])
        grad_real, grad_imag = grad_spec[:, 0], grad_spec[:, 1]
        in_real = backward_mix(grad_real, real_w) + backward_mix(grad_imag, imag_w)
        in_imag = backward_mix(grad_imag, real_w) - backward_mix(grad_real, imag_w)
        grad_spec_in = rounded(jnp.stack([in_real, in_imag], axis=1))
        grad_back_x = rounded(first_inverse(grad_spec_in))
        grad_fields = plane_inverse(grad_back_x, plain_weight).astype(jnp.bfloat16)
        term_real = outer_terms(real_in, grad_real) + outer_terms(imag_in, grad_imag)
        term_imag = outer_terms(real_in, grad_imag) - outer_terms(imag_in, grad_real)
        weight_term = rounded(jnp.stack([term_real, term_imag], axis=1).reshape(MX, 2, pairs, C * C))
        return carry + weight_term, grad_fields

    start = jnp.zeros((MX, 2, pairs, C * C), jnp.float32)
    grad_weight, grad_fields = lax.scan(one_sample, start, (fields, cotangent))
    return grad_fields, grad_weight
```

```python
import functools
import math

import jax
import jax.numpy as jnp
import numpy as np
from jax import lax
from jax.experimental import pallas as pl
from jax.experimental.pallas import tpu as pltpu
from jax.sharding import PartitionSpec as P

C = 32
MX = 32
MY = 32
MZ = 16
NX = 256
NY = 128
NZ = 32
PLANE = NY * NZ
PENCIL = 32
GROUPS = 8
XD = NX // PENCIL
ROWS = XD * C
SPEC = PENCIL * 2 * MZ
HALF = 128
CHUNKS = 4
MESH = pl.DeviceIdType.MESH
F32 = jnp.float32
BF16 = jnp.bfloat16

ERFCX = (
    0.1396285169187187,
    0.13968893082035916,
    0.12150772849569927,
    0.09702409559327627,
    0.001681622922537982,
    0.11598743251926187,
    -0.21153701193576485,
    0.11952101759674227,
    -0.02350221617294912,
)
DENSITY = 0.3989422804014327


def gelu_slope(v):
    a = jnp.abs(v)
    t = 1.0 / (1.0 + 0.35 * a)
    q = jnp.full_like(t, ERFCX[-1])
    for coef in ERFCX[-2::-1]:
        q = q * t + coef
    h = jnp.exp(-0.5 * v * v) * (q * t - DENSITY * a)
    return jnp.where(v >= 0.0, 1.0 - h, h)


@functools.lru_cache(None)
def tables():
    b = np.arange(MY)[:, None, None]
    c = np.arange(MZ)[None, :, None]
    p = np.arange(PLANE)[None, None, :]
    y, z = p % NY, p // NY
    turns = ((b - MY // 2) * y * (NZ // 1) + c * z * NY) % (NY * NZ)
    angle = turns * (2.0 * math.pi / (NY * NZ))
    plane = np.stack([np.cos(angle), -np.sin(angle)], axis=1).reshape(SPEC, PLANE)
    kx = np.arange(MX)[:, None] - MX // 2
    j = np.arange(ROWS)[None, :] // C
    phase = ((kx * j) % NX) * (2.0 * math.pi / NX)
    twiddle = np.stack([np.cos(phase), np.sin(phase)], axis=1)
    spread = np.zeros((HALF, C * C))
    spread[np.arange(C * C) // C, np.arange(C * C)] = 1.0
    gather = np.zeros((C * C, HALF))
    lane = np.arange(HALF)
    gather[:] = (np.arange(C * C)[:, None] // C) == (lane[None, :] % C)
    return (
        plane.astype(jnp.bfloat16),
        twiddle.astype(np.float32),
        spread.astype(jnp.bfloat16),
        gather.astype(jnp.bfloat16),
    )


def times(value, angle, sign):
    re, im = value
    if angle == 0:
        return value
    co, si = math.cos(2 * math.pi * angle), sign * math.sin(2 * math.pi * angle)
    if angle in (0.125, 0.375):
        root = math.sqrt(0.5)
        if angle == 0.125:
            if sign > 0:
                return (re - im) * root, (re + im) * root
            return (re + im) * root, (im - re) * root
        if sign > 0:
            return (re + im) * (-root), (re - im) * root
        return (im - re) * root, (re + im) * (-root)
    return re * co - im * si, re * si + im * co


def add(a, b):
    return a[0] + b[0], a[1] + b[1]


def sub(a, b):
    return a[0] - b[0], a[1] - b[1]


def fft(values, sign):
    n = len(values)
    if n == 1:
        return values
    even, odd = fft(values[0::2], sign), fft(values[1::2], sign)
    out = [None] * n
    for k in range(n // 2):
        if k * 4 == n:
            re, im = odd[k]
            turned = (-im, re) if sign > 0 else (im, -re)
        else:
            turned = times(odd[k], k / n, sign)
        out[k] = add(even[k], turned)
        out[k + n // 2] = sub(even[k], turned)
    return out


def dot(a, b, dims):
    return lax.dot_general(a, b, (dims, ((), ())), preferred_element_type=F32)


def kernel(
    x_hbm, cot_hbm, w_hbm, table_hbm, tw_ref, spread_ref, gather_ref,
    out_hbm, gw_hbm,
    x_ref, cot_ref, w_ref, table, send, recv, spec, grad, mixed, terms, acc, dx, dg, out_ref, gw_ref,
    load_sem, own_sem, send_sem, recv_sem, dp_send, dp_recv, dp_own, store_sem,
):
    me = lax.axis_index("pencil")
    group = lax.axis_index("dp")

    load_x = pltpu.make_async_copy(x_hbm, x_ref, load_sem.at[0])
    load_cot = pltpu.make_async_copy(cot_hbm, cot_ref, load_sem.at[1])
    load_w = pltpu.make_async_copy(w_hbm, w_ref, load_sem.at[2])
    chunk_rows = SPEC // CHUNKS
    chunk_peers = PENCIL // CHUNKS

    def chunk_of(step):
        return lax.rem(me // chunk_peers + step, CHUNKS)

    def load_table(step):
        rows = pl.ds(pl.multiple_of(chunk_of(step) * chunk_rows, chunk_rows), chunk_rows)
        return pltpu.make_async_copy(table_hbm.at[rows], table.at[rows], load_sem.at[3 + step])

    load_x.start()
    for step in range(CHUNKS):
        load_table(step).start()
    load_cot.start()
    load_w.start()

    barrier = pltpu.get_barrier_semaphore()

    def greet_pencil(i, carry):
        pl.semaphore_signal(
            barrier, inc=1, device_id=(group, lax.rem(me + i, PENCIL)), device_id_type=MESH
        )
        return carry

    def greet_group(i, carry):
        pl.semaphore_signal(
            barrier, inc=1, device_id=(lax.rem(group + i, GROUPS), me), device_id_type=MESH
        )
        return carry

    lax.fori_loop(1, PENCIL, greet_pencil, 0)
    lax.fori_loop(1, GROUPS, greet_group, 0)

    def post(phase, half, peer):
        pltpu.make_async_remote_copy(
            src_ref=send.at[phase, half, peer],
            dst_ref=recv.at[phase, half, me],
            send_sem=send_sem.at[phase, half],
            recv_sem=recv_sem.at[phase, half],
            device_id=(group, peer),
            device_id_type=MESH,
        ).start()

    def own_copy(phase, half):
        return pltpu.make_async_copy(
            send.at[phase, half, me], recv.at[phase, half, me], own_sem.at[phase, half]
        )

    def arrived(phase, half):
        block = recv.at[phase, half, pl.ds(0, PENCIL - 1)]
        pltpu.make_async_copy(block, block, recv_sem.at[phase, half]).wait()
        own_copy(phase, half).wait()

    def sent(phase, half):
        block = send.at[phase, half, pl.ds(0, PENCIL - 1)]
        pltpu.make_async_copy(block, block, send_sem.at[phase, half]).wait()

    def post_all(phase, half):
        def one(i, carry):
            post(phase, half, lax.rem(me + i, PENCIL))
            return carry

        lax.fori_loop(1, PENCIL, one, 0)
        own_copy(phase, half).start()

    def post_chunk(phase, half, chunk):
        def one(i, carry):
            peer = chunk * chunk_peers + lax.rem(me + i, chunk_peers)

            @pl.when(peer != me)
            def _():
                post(phase, half, peer)

            return carry

        lax.fori_loop(0, chunk_peers, one, 0)

    def plane_forward_chunk(source, phase, halves, chunk):
        rows = pl.ds(pl.multiple_of(chunk * chunk_rows, chunk_rows), chunk_rows)
        result = dot(table[rows, :], source, ((1,), (1,))).astype(BF16)
        for place, half in enumerate(halves):
            part = result[:, place * HALF : (place + 1) * HALF]
            send[phase, half, pl.ds(chunk * chunk_peers, chunk_peers)] = part.reshape(
                chunk_peers, 2, MZ, HALF
            )

    def first_forward(phase, half, scale, target):
        values = [
            (recv[phase, half, d, 0].astype(F32), recv[phase, half, d, 1].astype(F32))
            for d in range(PENCIL)
        ]
        spectrum = fft(values, -1)
        for a in range(MX):
            re, im = spectrum[(a - MX // 2) % MX]
            co = tw_ref[a, 0:1, half * HALF : (half + 1) * HALF]
            si = tw_ref[a, 1:2, half * HALF : (half + 1) * HALF]
            parts = (re * co + im * si, im * co - re * si)
            for r in range(2):
                if half == 0:
                    acc[a, r] = parts[r]
                else:
                    total = acc[a, r] + parts[r]
                    total = total + pltpu.roll(total, 64, 1)
                    total = total + pltpu.roll(total, 32, 1)
                    if scale is not None:
                        total = total * scale
                    target[a, r] = total.astype(BF16)

    def first_inverse(phase, half, scale):
        values = [None] * MX
        for a in range(MX):
            re, im = mixed[a, 0], mixed[a, 1]
            co = tw_ref[a, 0:1, half * HALF : (half + 1) * HALF]
            si = tw_ref[a, 1:2, half * HALF : (half + 1) * HALF]
            values[(a - MX // 2) % MX] = (re * co - im * si, im * co + re * si)
        signal = fft(values, 1)
        for d in range(PENCIL):
            for r in range(2):
                value = signal[d][r]
                if scale is not None:
                    value = value * scale
                send[phase, half, d, r] = value.astype(BF16)

    def share(source, target, which):
        def one(i, carry):
            peer = lax.rem(group + i, GROUPS)
            pltpu.make_async_remote_copy(
                src_ref=source.at[pl.ds(peer * (MX // GROUPS), MX // GROUPS)],
                dst_ref=target.at[group],
                send_sem=dp_send.at[which],
                recv_sem=dp_recv.at[which],
                device_id=(peer, me),
                device_id_type=MESH,
            ).start()
            return carry

        lax.fori_loop(1, GROUPS, one, 0)
        share_own(source, target, which).start()

    def share_own(source, target, which):
        return pltpu.make_async_copy(
            source.at[pl.ds(group * (MX // GROUPS), MX // GROUPS)],
            target.at[group],
            dp_own.at[which],
        )

    def shared(source, target, which):
        block = target.at[pl.ds(0, GROUPS - 1)]
        pltpu.make_async_copy(block, block, dp_recv.at[which]).wait()
        pltpu.make_async_copy(block, block, dp_send.at[which]).wait()
        share_own(source, target, which).wait()

    depth = lax.broadcasted_iota(jnp.int32, (MZ, HALF), 0)
    mode_scale = jnp.where(depth == 0, 1.0, 2.0).astype(F32) * (1.0 / (NX * NY * NZ))

    load_x.wait()
    for step in range(CHUNKS):
        load_table(step).wait()
        chunk = chunk_of(step)
        plane_forward_chunk(x_ref[...], 0, (0, 1), chunk)
        if step == 0:
            pl.semaphore_wait(barrier, PENCIL + GROUPS - 2)
        for half in range(2):
            post_chunk(0, half, chunk)
    for half in range(2):
        own_copy(0, half).start()
    load_w.wait()
    load_cot.wait()
    for half in range(2):
        arrived(0, half)
        first_forward(0, half, None, spec)
    share(spec, dx, 0)

    block_a = 4

    def forward_mix(step, carry):
        a0 = step * block_a
        lines = spec[pl.ds(a0, block_a)].reshape(block_a * 2 * MZ, HALF)
        wide = dot(lines, spread_ref[...], ((1,), (0,))).reshape(block_a, 2, MZ, C * C)
        for a in range(block_a):
            out_re = jnp.zeros((MZ, HALF), F32)
            out_im = jnp.zeros((MZ, HALF), F32)
            for t in range(C * C // HALF):
                lanes = slice(t * HALF, (t + 1) * HALF)
                w_re = w_ref[a0 + a, 0, :, lanes].astype(F32)
                w_im = w_ref[a0 + a, 1, :, lanes].astype(F32)
                x_re, x_im = wide[a, 0, :, lanes], wide[a, 1, :, lanes]
                out_re = out_re + x_re * w_re - x_im * w_im
                out_im = out_im + x_re * w_im + x_im * w_re
            for r, total in enumerate((out_re, out_im)):
                total = total + pltpu.roll(total, 64, 1)
                total = total + pltpu.roll(total, 32, 1)
                mixed[a0 + a, r] = total.astype(BF16).astype(F32)
        return carry

    lax.fori_loop(0, MX // block_a, forward_mix, 0)

    for half in range(2):
        first_inverse(1, half, mode_scale)
        post_all(1, half)

    width = 512
    for half in range(2):
        arrived(1, half)
        lines = recv[1, half].reshape(SPEC, HALF).T
        rows = pl.ds(half * HALF, HALF)

        def cells(step, carry):
            lanes = pl.ds(pl.multiple_of(step * width, width), width)
            pre = dot(lines, table[:, lanes], ((1,), (0,)))
            slope = gelu_slope(pre) * cot_ref[rows, lanes].astype(F32)
            grad[rows, lanes] = slope.astype(BF16)
            return carry

        lax.fori_loop(0, PLANE // width, cells, 0)
        for step in range(CHUNKS):
            chunk = chunk_of(step)
            plane_forward_chunk(grad[rows, :], 2, (half,), chunk)
            post_chunk(2, half, chunk)
        own_copy(2, half).start()

    for half in range(2):
        arrived(2, half)
        first_forward(2, half, mode_scale, terms)
    share(terms, dg, 1)

    def backward_mix(step, carry):
        a0 = step * block_a
        for a in range(block_a):
            g_re, g_im = terms[a0 + a, 0].astype(F32), terms[a0 + a, 1].astype(F32)
            parts_re, parts_im = [], []
            for t in range(C * C // HALF):
                lanes = slice(t * HALF, (t + 1) * HALF)
                w_re = w_ref[a0 + a, 0, :, lanes].astype(F32)
                w_im = w_ref[a0 + a, 1, :, lanes].astype(F32)
                parts_re.append((g_re * w_re + g_im * w_im).astype(BF16))
                parts_im.append((g_im * w_re - g_re * w_im).astype(BF16))
            both = jnp.concatenate(
                [jnp.concatenate(parts_re, axis=1), jnp.concatenate(parts_im, axis=1)], axis=0
            )
            sums = dot(both, gather_ref[...], ((1,), (0,))).astype(BF16).astype(F32)
            mixed[a0 + a] = sums.reshape(2, MZ, HALF)
        return carry

    lax.fori_loop(0, MX // block_a, backward_mix, 0)

    for half in range(2):
        first_inverse(3, half, None)
        post_all(3, half)

    shared(spec, dx, 0)
    shared(terms, dg, 1)

    def outer(a, carry):
        lines = jnp.concatenate([dx[s, a].reshape(2 * MZ, HALF) for s in range(GROUPS)], axis=0)
        wide = dot(lines, spread_ref[...], ((1,), (0,))).reshape(GROUPS, 2, MZ, C * C)
        g = [(dg[s, a, 0].astype(F32), dg[s, a, 1].astype(F32)) for s in range(GROUPS)]
        for t in range(C * C // HALF):
            lanes = slice(t * HALF, (t + 1) * HALF)
            out_re = jnp.zeros((MZ, HALF), F32)
            out_im = jnp.zeros((MZ, HALF), F32)
            for s in range(GROUPS):
                x_re, x_im = wide[s, 0, :, lanes], wide[s, 1, :, lanes]
                out_re = out_re + x_re * g[s][0] + x_im * g[s][1]
                out_im = out_im + x_re * g[s][1] - x_im * g[s][0]
            gw_ref[a, 0, :, lanes] = out_re
            gw_ref[a, 1, :, lanes] = out_im
        return carry

    lax.fori_loop(0, MX // GROUPS, outer, 0)
    store_gw = pltpu.make_async_copy(gw_ref, gw_hbm, store_sem.at[2])
    store_gw.start()

    for half in range(2):
        arrived(3, half)
        lines = recv[3, half].reshape(SPEC, HALF).T
        rows = pl.ds(half * HALF, HALF)

        def finish(step, carry):
            lanes = pl.ds(pl.multiple_of(step * width, width), width)
            out_ref[rows, lanes] = dot(lines, table[:, lanes], ((1,), (0,))).astype(BF16)
            return carry

        lax.fori_loop(0, PLANE // width, finish, 0)
        pltpu.make_async_copy(out_ref.at[rows], out_hbm.at[rows], store_sem.at[half]).start()

    for phase in range(4):
        for half in range(2):
            sent(phase, half)
    for half in range(2):
        rows = pl.ds(half * HALF, HALF)
        pltpu.make_async_copy(out_ref.at[rows], out_hbm.at[rows], store_sem.at[half]).wait()
    store_gw.wait()


def per_device(fields, cotangent, spectral_weight):
    plane, twiddle, spread, gather = tables()
    any_space = pl.BlockSpec(memory_space=pl.ANY)
    vmem = pl.BlockSpec(memory_space=pltpu.VMEM)
    block = (PENCIL, 2, MZ, HALF)
    spectrum = (MX, 2, MZ, HALF)
    mine = MX // GROUPS
    grad_fields, grad_weight = pl.pallas_call(
        kernel,
        out_shape=(
            jax.ShapeDtypeStruct((ROWS, PLANE), BF16),
            jax.ShapeDtypeStruct((mine, 2, MZ, C * C), F32),
        ),
        in_specs=[any_space] * 4 + [vmem] * 3,
        out_specs=(any_space, any_space),
        scratch_shapes=[
            pltpu.VMEM((ROWS, PLANE), BF16),
            pltpu.VMEM((ROWS, PLANE), BF16),
            pltpu.VMEM((MX, 2, MZ, C * C), BF16),
            pltpu.VMEM((SPEC, PLANE), BF16),
            pltpu.VMEM((4, 2) + block, BF16),
            pltpu.VMEM((4, 2) + block, BF16),
            pltpu.VMEM(spectrum, BF16),
            pltpu.VMEM((ROWS, PLANE), BF16),
            pltpu.VMEM(spectrum, F32),
            pltpu.VMEM(spectrum, BF16),
            pltpu.VMEM(spectrum, F32),
            pltpu.VMEM((GROUPS, mine, 2, MZ, HALF), BF16),
            pltpu.VMEM((GROUPS, mine, 2, MZ, HALF), BF16),
            pltpu.VMEM((ROWS, PLANE), BF16),
            pltpu.VMEM((mine, 2, MZ, C * C), F32),
            pltpu.SemaphoreType.DMA((3 + CHUNKS,)),
            pltpu.SemaphoreType.DMA((4, 2)),
            pltpu.SemaphoreType.DMA((4, 2)),
            pltpu.SemaphoreType.DMA((4, 2)),
            pltpu.SemaphoreType.DMA((2,)),
            pltpu.SemaphoreType.DMA((2,)),
            pltpu.SemaphoreType.DMA((2,)),
            pltpu.SemaphoreType.DMA((3,)),
        ],
        compiler_params=pltpu.CompilerParams(
            collective_id=0, has_side_effects=True, vmem_limit_bytes=56 * 2**20
        ),
        cost_estimate=pl.CostEstimate(flops=9 * 10**9, bytes_accessed=20 * 2**20, transcendentals=2**21),
    )(
        fields.reshape(ROWS, PLANE),
        cotangent.reshape(ROWS, PLANE),
        spectral_weight,
        jnp.asarray(plane),
        jnp.asarray(twiddle),
        jnp.asarray(spread),
        jnp.asarray(gather),
    )
    return grad_fields.reshape(1, XD, C, PLANE), grad_weight


def solution(mesh):
    placed = (
        P("dp", "pencil", None, None),
        P("dp", "pencil", None, None),
        P(None, None, "pencil", None),
    )
    return jax.shard_map(
        per_device,
        mesh=mesh,
        in_specs=placed,
        out_specs=(P("dp", "pencil", None, None), P("dp", None, "pencil", None)),
        check_vma=False,
    )
```

```python
import functools
import math

import jax
import jax.numpy as jnp
import numpy as np
from jax import lax
from jax.experimental import pallas as pl
from jax.experimental.pallas import tpu as pltpu
from jax.sharding import PartitionSpec as P

C = 32
MX = 32
MY = 32
MZ = 16
NX = 256
NY = 128
NZ = 32
PLANE = NY * NZ
PENCIL = 32
GROUPS = 8
XD = NX // PENCIL
ROWS = XD * C
SPEC = PENCIL * 2 * MZ
HALF = 128
FOLD = PLANE // 2
DEEP = MZ // 2
STACKS = 8
CORES = PENCIL // STACKS
MESH = pl.DeviceIdType.MESH
F32 = jnp.float32
BF16 = jnp.bfloat16

ROOT_HALF = 0.7071067811865476
DENSITY = 0.3989422804014327


def gelu_slope(v):
    return 0.5 * (1.0 + lax.erf(v * ROOT_HALF)) + v * jnp.exp(-0.5 * v * v) * DENSITY


@functools.lru_cache(None)
def tables():
    b = np.arange(MY)[None, :, None, None]
    c = 2 * np.arange(DEEP)[None, None, :, None] + np.arange(2)[:, None, None, None]
    p = np.arange(FOLD)[None, None, None, :]
    y, z = p % NY, p // NY
    turns = ((b - MY // 2) * y * NZ + c * z * NY) % PLANE
    angle = turns * (2.0 * math.pi / PLANE)
    plane = np.stack([np.cos(angle), -np.sin(angle)], axis=2).reshape(2, SPEC // 2, FOLD)
    kx = np.arange(MX)[:, None] - MX // 2
    j = np.arange(ROWS)[None, :] // C
    phase = ((kx * j) % NX) * (2.0 * math.pi / NX)
    twiddle = np.stack([np.cos(phase), np.sin(phase)], axis=1)
    lane = np.arange(HALF)
    pairs = np.arange(C * C)
    wide = (lane[:, None] % C) == (pairs[None, :] // C)
    again = (lane[:, None] % C) == (lane[None, :] % C)
    spread = np.tile(np.concatenate([wide, again], axis=1), (2, 1))
    first = wide * (lane[:, None] < C)
    gather = (pairs[:, None] // C) == (lane[None, :] % C)
    order = np.arange(HALF).reshape(4, 2, DEEP, 2).transpose(3, 0, 1, 2).reshape(-1)
    parity = np.zeros((HALF, HALF))
    parity[np.arange(HALF), order] = 1.0
    return (
        plane.astype(jnp.bfloat16),
        twiddle.astype(np.float32),
        spread.astype(jnp.bfloat16),
        first.astype(jnp.bfloat16),
        gather.astype(jnp.bfloat16),
        parity.astype(jnp.bfloat16),
    )


def times(value, angle, sign):
    re, im = value
    if angle == 0:
        return value
    co, si = math.cos(2 * math.pi * angle), sign * math.sin(2 * math.pi * angle)
    if angle in (0.125, 0.375):
        root = math.sqrt(0.5)
        if angle == 0.125:
            if sign > 0:
                return (re - im) * root, (re + im) * root
            return (re + im) * root, (im - re) * root
        if sign > 0:
            return (re + im) * (-root), (re - im) * root
        return (im - re) * root, (re + im) * (-root)
    return re * co - im * si, re * si + im * co


def add(a, b):
    return a[0] + b[0], a[1] + b[1]


def sub(a, b):
    return a[0] - b[0], a[1] - b[1]


def fft(values, sign):
    n = len(values)
    if n == 1:
        return values
    even, odd = fft(values[0::2], sign), fft(values[1::2], sign)
    out = [None] * n
    for k in range(n // 2):
        if k * 4 == n:
            re, im = odd[k]
            turned = (-im, re) if sign > 0 else (im, -re)
        else:
            turned = times(odd[k], k / n, sign)
        out[k] = add(even[k], turned)
        out[k + n // 2] = sub(even[k], turned)
    return out


def dot(a, b, dims):
    return lax.dot_general(a, b, (dims, ((), ())), preferred_element_type=F32)


def halves(value):
    high = value.astype(BF16)
    low = (value - high.astype(F32)).astype(BF16)
    return jnp.concatenate([high, low], axis=1)


def kernel(
    x_hbm, cot_hbm, w_hbm, table_hbm, tw_hbm, spread_hbm, first_hbm, gather_hbm, parity_hbm,
    out_hbm, gw_hbm,
    x_ref, cot_ref, w_ref, table, tw_ref, spread_ref, first_ref, gather_ref, parity_ref,
    send, recv, folded, even, weight, acc, spec, terms, mixed, dx, dg, out_ref, gw_ref,
    load_sem, own_sem, send_sem, recv_sem, dp_send, dp_recv, dp_own, store_sem,
):
    me = lax.axis_index("pencil")
    group = lax.axis_index("dp")
    stack, core = me // CORES, lax.rem(me, CORES)

    loads = [
        pltpu.make_async_copy(source, target, load_sem.at[place])
        for place, (source, target) in enumerate(
            [
                (x_hbm, x_ref),
                (table_hbm.at[0], table.at[0]),
                (table_hbm.at[1], table.at[1]),
                (parity_hbm, parity_ref),
                (w_hbm, w_ref),
                (tw_hbm, tw_ref),
                (spread_hbm, spread_ref),
                (gather_hbm, gather_ref),
                (first_hbm, first_ref),
                (cot_hbm, cot_ref),
            ]
        )
    ]
    for load in loads:
        load.start()

    barrier = pltpu.get_barrier_semaphore()

    def greet_pencil(i, carry):
        pl.semaphore_signal(
            barrier, inc=1, device_id=(group, lax.rem(me + i, PENCIL)), device_id_type=MESH
        )
        return carry

    def greet_group(i, carry):
        pl.semaphore_signal(
            barrier, inc=1, device_id=(lax.rem(group + i, GROUPS), me), device_id_type=MESH
        )
        return carry

    lax.fori_loop(1, PENCIL, greet_pencil, 0)
    lax.fori_loop(1, GROUPS, greet_group, 0)

    def block(ref, phase, parity, part, places):
        if part is None:
            return ref.at[phase, parity, places]
        return ref.at[phase, parity, places, part]

    def post(phase, parity, part, peer):
        slot = part or 0
        pltpu.make_async_remote_copy(
            src_ref=block(send, phase, parity, part, peer),
            dst_ref=block(recv, phase, parity, part, me),
            send_sem=send_sem.at[phase, parity, slot],
            recv_sem=recv_sem.at[phase, parity, slot],
            device_id=(group, peer),
            device_id_type=MESH,
        ).start()

    def own_copy(phase, parity, part):
        return pltpu.make_async_copy(
            block(send, phase, parity, part, me),
            block(recv, phase, parity, part, me),
            own_sem.at[phase, parity, part or 0],
        )

    def arrived(phase, parity, part):
        whole = block(recv, phase, parity, part, pl.ds(0, PENCIL - 1))
        pltpu.make_async_copy(whole, whole, recv_sem.at[phase, parity, part or 0]).wait()
        own_copy(phase, parity, part).wait()

    def sent(phase, parity, part):
        whole = block(send, phase, parity, part, pl.ds(0, PENCIL - 1))
        pltpu.make_async_copy(whole, whole, send_sem.at[phase, parity, part or 0]).wait()

    def stack_at(step):
        offset = STACKS // 2 + ((step + 1) // 2) * (2 * lax.rem(step, 2) - 1)
        return lax.rem(stack + offset + STACKS, STACKS)

    def post_stacks(phase, parity, part, steps):
        def one(i, carry):
            peer = stack_at(i // CORES) * CORES + lax.rem(core + i, CORES)

            @pl.when(peer != me)
            def _():
                post(phase, parity, part, peer)

            return carry

        lax.fori_loop(steps[0] * CORES, steps[1] * CORES, one, 0)

    def post_all(phase, parity, part):
        post_stacks(phase, parity, part, (0, STACKS))
        own_copy(phase, parity, part).start()

    lines_stack = CORES * 2 * DEEP

    def plane_forward(source, phase, parity, part, before_post=None):
        pieces = 2
        each = STACKS // pieces
        for piece in range(pieces):
            stacks = [stack_at(jnp.int32(piece * each + k)) for k in range(each)]
            lines = jnp.concatenate(
                [
                    table[parity, pl.ds(pl.multiple_of(at * lines_stack, lines_stack), lines_stack)]
                    for at in stacks
                ],
                axis=0,
            )
            result = dot(lines, source, ((1,), (1,))).astype(BF16)
            for k, at in enumerate(stacks):
                mine = result[k * lines_stack : (k + 1) * lines_stack]
                places = pl.ds(at * CORES, CORES)
                for place, half in enumerate((0, 1) if part is None else (part,)):
                    send[phase, parity, places, half] = mine[
                        :, place * HALF : (place + 1) * HALF
                    ].reshape(CORES, 2 * DEEP, HALF)
            if before_post is not None and piece == 0:
                before_post()
            post_stacks(phase, parity, part, (piece * each, (piece + 1) * each))
        own_copy(phase, parity, part).start()

    def first_forward(phase, parity, half):
        values = []
        for d in range(PENCIL):
            both = recv[phase, parity, d, half].astype(F32)
            values.append((both[:DEEP], both[DEEP:]))
        spectrum = fft(values, -1)
        for a in range(MX):
            re, im = spectrum[(a - MX // 2) % MX]
            co = tw_ref[a, 0:1, half * HALF : (half + 1) * HALF]
            si = tw_ref[a, 1:2, half * HALF : (half + 1) * HALF]
            for r, value in enumerate((re * co + im * si, im * co - re * si)):
                rows = slice(r * DEEP, (r + 1) * DEEP)
                acc[parity, a, rows] = value if half == 0 else acc[parity, a, rows] + value

    def first_inverse(phase, parity, half, scale):
        values = [None] * MX
        for a in range(MX):
            re, im = mixed[a, :DEEP], mixed[a, DEEP:]
            co = tw_ref[a, 0:1, half * HALF : (half + 1) * HALF]
            si = tw_ref[a, 1:2, half * HALF : (half + 1) * HALF]
            values[(a - MX // 2) % MX] = (re * co - im * si, im * co + re * si)
        signal = fft(values, 1)
        for d in range(PENCIL):
            both = jnp.concatenate(signal[d], axis=0)
            if scale is not None:
                both = both * scale
            send[phase, parity, d, half] = both.astype(BF16)

    def share_own(source, target, which):
        return pltpu.make_async_copy(
            source.at[pl.ds(group * (MX // GROUPS), MX // GROUPS)],
            target.at[group],
            dp_own.at[which],
        )

    def share(source, target, which):
        def one(i, carry):
            peer = lax.rem(group + i, GROUPS)
            pltpu.make_async_remote_copy(
                src_ref=source.at[pl.ds(peer * (MX // GROUPS), MX // GROUPS)],
                dst_ref=target.at[group],
                send_sem=dp_send.at[which],
                recv_sem=dp_recv.at[which],
                device_id=(peer, me),
                device_id_type=MESH,
            ).start()
            return carry

        lax.fori_loop(1, GROUPS, one, 0)
        share_own(source, target, which).start()

    def shared(source, target, which):
        whole = target.at[pl.ds(0, GROUPS - 1)]
        pltpu.make_async_copy(whole, whole, dp_recv.at[which]).wait()
        pltpu.make_async_copy(whole, whole, dp_send.at[which]).wait()
        share_own(source, target, which).wait()

    depth = lax.rem(lax.broadcasted_iota(jnp.int32, (2 * DEEP, HALF), 0), DEEP)
    volume = 1.0 / (NX * NY * NZ)
    scales = (
        jnp.where(depth == 0, volume, 2.0 * volume).astype(F32),
        jnp.full((2 * DEEP, HALF), 2.0 * volume, F32),
    )
    block_a = 8
    block_rows = block_a * 2 * DEEP
    lane_tiles = [slice(t * HALF, (t + 1) * HALF) for t in range(C * C // HALF)]

    def forward_mix(parity):
        def one(step, carry):
            own_a = pl.ds(step * block_a, block_a)
            lines = halves(acc[parity, own_a].reshape(block_rows, HALF))
            wide = dot(lines, spread_ref[...], ((1,), (0,)))
            spec[own_a, parity] = (
                wide[:, C * C :].astype(BF16).reshape(block_a, 2 * DEEP, HALF)
            )
            totals = []
            for a in range(block_a):
                out_re = jnp.zeros((DEEP, HALF), F32)
                out_im = jnp.zeros((DEEP, HALF), F32)
                row = a * 2 * DEEP
                for lanes in lane_tiles:
                    w_re = weight[parity, step * block_a + a, :DEEP, lanes]
                    w_im = weight[parity, step * block_a + a, DEEP:, lanes]
                    x_re = wide[row : row + DEEP, lanes]
                    x_im = wide[row + DEEP : row + 2 * DEEP, lanes]
                    out_re = out_re + x_re * w_re - x_im * w_im
                    out_im = out_im + x_re * w_im + x_im * w_re
                totals += [out_re, out_im]
            sums = dot(halves(jnp.concatenate(totals, axis=0)), spread_ref[:, C * C :], ((1,), (0,)))
            mixed[own_a] = sums.reshape(block_a, 2 * DEEP, HALF)
            return carry

        lax.fori_loop(0, MX // block_a, one, 0)

    def backward_mix(parity):
        def one(step, carry):
            own_a = pl.ds(step * block_a, block_a)
            lines = halves(acc[parity, own_a].reshape(block_rows, HALF))
            sums = dot(lines, spread_ref[:, C * C :], ((1,), (0,)))
            narrow = (sums.reshape(block_a, 2 * DEEP, HALF) * scales[parity]).astype(BF16)
            terms[own_a, parity] = narrow
            grads = narrow.astype(F32)
            products = []
            for a in range(block_a):
                g_re, g_im = grads[a, :DEEP], grads[a, DEEP:]
                tiles = []
                for lanes in lane_tiles:
                    w_re = weight[parity, step * block_a + a, :DEEP, lanes]
                    w_im = weight[parity, step * block_a + a, DEEP:, lanes]
                    tiles.append(
                        jnp.concatenate(
                            [g_re * w_re + g_im * w_im, g_im * w_re - g_re * w_im], axis=0
                        ).astype(BF16)
                    )
                products.append(jnp.concatenate(tiles, axis=1))
            result = dot(jnp.concatenate(products, axis=0), gather_ref[...], ((1,), (0,)))
            mixed[own_a] = result.reshape(block_a, 2 * DEEP, HALF)
            return carry

        lax.fori_loop(0, MX // block_a, one, 0)

    width = 512

    def lines_of(phase, parity, half):
        return recv[phase, parity, :, half].reshape(SPEC // 2, HALF)

    def even_cells(phase):
        lines = jnp.concatenate([lines_of(phase, 0, 0), lines_of(phase, 0, 1)], axis=1).T

        def one(step, carry):
            lanes = pl.ds(pl.multiple_of(step * width, width), width)
            even[:, lanes] = dot(lines, table[0, :, lanes], ((1,), (0,)))
            return carry

        lax.fori_loop(0, FOLD // width, one, 0)

    def odd_cells(phase, half, finish):
        lines = lines_of(phase, 1, half).T
        rows = pl.ds(half * HALF, HALF)

        def one(step, carry):
            near = pl.ds(pl.multiple_of(step * width, width), width)
            far = pl.ds(pl.multiple_of(FOLD + step * width, width), width)
            odd = dot(lines, table[1, :, near], ((1,), (0,)))
            base = even[rows, near]
            finish(rows, near, far, base + odd, base - odd)
            return carry

        lax.fori_loop(0, FOLD // width, one, 0)

    loads[0].wait()

    def fold_fields(step, carry):
        near = pl.ds(pl.multiple_of(step * width, width), width)
        far = pl.ds(pl.multiple_of(FOLD + step * width, width), width)
        one, two = x_ref[:, near].astype(F32), x_ref[:, far].astype(F32)
        folded[0, :, near] = (one + two).astype(BF16)
        folded[1, :, near] = (one - two).astype(BF16)
        return carry

    lax.fori_loop(0, FOLD // width, fold_fields, 0)
    loads[1].wait()

    def all_here():
        pl.semaphore_wait(barrier, PENCIL + GROUPS - 2)

    plane_forward(folded[0], 0, 0, None, all_here)
    loads[2].wait()
    plane_forward(folded[1], 0, 1, None)

    loads[3].wait()
    loads[4].wait()

    def part_weights(step, carry):
        own_a = pl.ds(step * 4, 4)
        lines = w_ref[own_a].reshape(HALF, C * C)
        apart = dot(parity_ref[...], lines, ((1,), (0,)))
        for parity in range(2):
            weight[parity, own_a] = apart[parity * HALF // 2 : (parity + 1) * HALF // 2].reshape(
                4, 2 * DEEP, C * C
            )
        return carry

    lax.fori_loop(0, MX // 4, part_weights, 0)
    for load in loads[5:]:
        load.wait()

    for parity in range(2):
        arrived(0, parity, None)
        for half in range(2):
            first_forward(0, parity, half)
        forward_mix(parity)
        for half in range(2):
            first_inverse(1, parity, half, scales[parity])
            if parity == 1:
                post_all(1, parity, half)
        if parity == 0:
            post_all(1, parity, None)
    share(spec, dx, 0)

    arrived(1, 0, None)
    even_cells(1)

    def slopes(rows, near, far, one, two):
        one = gelu_slope(one) * cot_ref[rows, near].astype(F32)
        two = gelu_slope(two) * cot_ref[rows, far].astype(F32)
        folded[0, rows, near] = (one + two).astype(BF16)
        folded[1, rows, near] = (one - two).astype(BF16)

    for half in range(2):
        arrived(1, 1, half)
        odd_cells(1, half, slopes)
        for parity in range(2):
            plane_forward(folded[parity, pl.ds(half * HALF, HALF)], 2, parity, half)

    for parity in range(2):
        arrived(2, parity, 0)
        first_forward(2, parity, 0)
    for parity in range(2):
        arrived(2, parity, 1)
        first_forward(2, parity, 1)
        backward_mix(parity)
        for half in range(2):
            first_inverse(3, parity, half, None)
            if parity == 1:
                post_all(3, parity, half)
        if parity == 0:
            post_all(3, parity, None)
    share(terms, dg, 1)

    shared(spec, dx, 0)
    shared(terms, dg, 1)

    def outer(a, carry):
        for parity in range(2):
            lines = jnp.concatenate([dx[s, a, parity] for s in range(GROUPS)], axis=0)
            wide = dot(lines, first_ref[...], ((1,), (0,)))
            factors = [dg[s, a, parity].astype(F32) for s in range(GROUPS)]
            for tile, lanes in enumerate(lane_tiles):
                out_re = jnp.zeros((DEEP, HALF), F32)
                out_im = jnp.zeros((DEEP, HALF), F32)
                for s in range(GROUPS):
                    row = s * 2 * DEEP
                    x_re, x_im = wide[row : row + DEEP, lanes], wide[row + DEEP : row + 2 * DEEP, lanes]
                    g_re, g_im = factors[s][:DEEP], factors[s][DEEP:]
                    out_re = out_re + x_re * g_re + x_im * g_im
                    out_im = out_im + x_re * g_im - x_im * g_re
                gw_ref[tile, a, 0, pl.ds(parity, DEEP, stride=2)] = out_re
                gw_ref[tile, a, 1, pl.ds(parity, DEEP, stride=2)] = out_im
        return carry

    lax.fori_loop(0, MX // GROUPS, outer, 0)
    stores = [
        pltpu.make_async_copy(gw_ref.at[tile], gw_hbm.at[:, :, :, lanes], store_sem.at[2 + tile])
        for tile, lanes in enumerate(lane_tiles)
    ]
    for store in stores:
        store.start()

    arrived(3, 0, None)
    even_cells(3)

    def finish(rows, near, far, one, two):
        out_ref[rows, near] = one.astype(BF16)
        out_ref[rows, far] = two.astype(BF16)

    for half in range(2):
        rows = pl.ds(half * HALF, HALF)
        arrived(3, 1, half)
        odd_cells(3, half, finish)
        pltpu.make_async_copy(out_ref.at[rows], out_hbm.at[rows], store_sem.at[half]).start()

    for parity in range(2):
        sent(0, parity, None)
        for half in range(2):
            sent(2, parity, half)
    for phase in (1, 3):
        sent(phase, 0, None)
        for half in range(2):
            sent(phase, 1, half)
    for half in range(2):
        rows = pl.ds(half * HALF, HALF)
        pltpu.make_async_copy(out_ref.at[rows], out_hbm.at[rows], store_sem.at[half]).wait()
    for store in stores:
        store.wait()


def per_device(fields, cotangent, spectral_weight):
    any_space = pl.BlockSpec(memory_space=pl.ANY)
    messages = (4, 2, PENCIL, 2, 2 * DEEP, HALF)
    spectrum = (MX, 2, 2 * DEEP, HALF)
    mine = MX // GROUPS
    constants = [jnp.asarray(table) for table in tables()]
    grad_fields, grad_weight = pl.pallas_call(
        kernel,
        out_shape=(
            jax.ShapeDtypeStruct((ROWS, PLANE), BF16),
            jax.ShapeDtypeStruct((mine, 2, MZ, C * C), F32),
        ),
        in_specs=[any_space] * (3 + len(constants)),
        out_specs=(any_space, any_space),
        scratch_shapes=[
            pltpu.VMEM((ROWS, PLANE), BF16),
            pltpu.VMEM((ROWS, PLANE), BF16),
            pltpu.VMEM((MX, 2, MZ, C * C), BF16),
        ]
        + [pltpu.VMEM(table.shape, table.dtype) for table in constants]
        + [
            pltpu.VMEM(messages, BF16),
            pltpu.VMEM(messages, BF16),
            pltpu.VMEM((2, ROWS, FOLD), BF16),
            pltpu.VMEM((ROWS, FOLD), F32),
            pltpu.VMEM((2, MX, 2 * DEEP, C * C), F32),
            pltpu.VMEM((2, MX, 2 * DEEP, HALF), F32),
            pltpu.VMEM(spectrum, BF16),
            pltpu.VMEM(spectrum, BF16),
            pltpu.VMEM((MX, 2 * DEEP, HALF), F32),
            pltpu.VMEM((GROUPS, mine, 2, 2 * DEEP, HALF), BF16),
            pltpu.VMEM((GROUPS, mine, 2, 2 * DEEP, HALF), BF16),
            pltpu.VMEM((ROWS, PLANE), BF16),
            pltpu.VMEM((C * C // HALF, mine, 2, MZ, HALF), F32),
            pltpu.SemaphoreType.DMA((10,)),
            pltpu.SemaphoreType.DMA((4, 2, 2)),
            pltpu.SemaphoreType.DMA((4, 2, 2)),
            pltpu.SemaphoreType.DMA((4, 2, 2)),
            pltpu.SemaphoreType.DMA((2,)),
            pltpu.SemaphoreType.DMA((2,)),
            pltpu.SemaphoreType.DMA((2,)),
            pltpu.SemaphoreType.DMA((2 + C * C // HALF,)),
        ],
        compiler_params=pltpu.CompilerParams(
            collective_id=0, has_side_effects=True, vmem_limit_bytes=60 * 2**20
        ),
        cost_estimate=pl.CostEstimate(
            flops=5 * 10**9, bytes_accessed=16 * 2**20, transcendentals=2**21
        ),
    )(
        fields.reshape(ROWS, PLANE),
        cotangent.reshape(ROWS, PLANE),
        spectral_weight,
        *constants,
    )
    return grad_fields.reshape(1, XD, C, PLANE), grad_weight


def solution(mesh):
    placed = (
        P("dp", "pencil", None, None),
        P("dp", "pencil", None, None),
        P(None, None, "pencil", None),
    )
    return jax.shard_map(
        per_device,
        mesh=mesh,
        in_specs=placed,
        out_specs=(P("dp", "pencil", None, None), P("dp", None, "pencil", None)),
        check_vma=False,
    )
```

```python
import functools
import math

import jax
import jax.numpy as jnp
import numpy as np
from jax import lax
from jax.experimental import pallas as pl
from jax.experimental.pallas import tpu as pltpu
from jax.sharding import PartitionSpec as P

C = 32
MX = 32
MY = 32
MZ = 16
NX = 256
NY = 128
NZ = 32
PLANE = NY * NZ
PENCIL = 32
GROUPS = 8
XD = NX // PENCIL
ROWS = XD * C
SPEC = PENCIL * 2 * MZ
HALF = 128
FOLD = PLANE // 2
DEEP = MZ // 2
STORES = 16
STACKS = 8
CORES = PENCIL // STACKS
MESH = pl.DeviceIdType.MESH
F32 = jnp.float32
BF16 = jnp.bfloat16

ROOT_HALF = 0.7071067811865476
DENSITY = 0.3989422804014327


def gelu_slope(v):
    return 0.5 * (1.0 + lax.erf(v * ROOT_HALF)) + v * jnp.exp(-0.5 * v * v) * DENSITY


@functools.lru_cache(None)
def tables():
    b = np.arange(MY)[None, :, None, None]
    c = 2 * np.arange(DEEP)[None, None, :, None] + np.arange(2)[:, None, None, None]
    p = np.arange(FOLD)[None, None, None, :]
    y, z = p % NY, p // NY
    turns = ((b - MY // 2) * y * NZ + c * z * NY) % PLANE
    angle = turns * (2.0 * math.pi / PLANE)
    plane = np.stack([np.cos(angle), -np.sin(angle)], axis=2).reshape(2, SPEC // 2, FOLD)
    kx = np.arange(MX)[:, None] - MX // 2
    j = np.arange(ROWS)[None, :] // C
    phase = ((kx * j) % NX) * (2.0 * math.pi / NX)
    twiddle = np.stack([np.cos(phase), np.sin(phase)], axis=1)
    lane = np.arange(HALF)
    pairs = np.arange(C * C)
    wide = (lane[:, None] % C) == (pairs[None, :] // C)
    again = (lane[:, None] % C) == (lane[None, :] % C)
    spread = np.tile(np.concatenate([wide, again], axis=1), (2, 1))
    first = wide * (lane[:, None] < C)
    gather = (pairs[:, None] // C) == (lane[None, :] % C)
    order = np.arange(HALF).reshape(4, 2, DEEP, 2).transpose(3, 0, 1, 2).reshape(-1)
    parity = np.zeros((HALF, HALF))
    parity[np.arange(HALF), order] = 1.0
    return (
        plane.astype(jnp.bfloat16),
        twiddle.astype(np.float32),
        spread.astype(jnp.bfloat16),
        first.astype(jnp.bfloat16),
        gather.astype(jnp.bfloat16),
        parity.astype(jnp.bfloat16),
    )


def times(value, angle, sign):
    re, im = value
    if angle == 0:
        return value
    co, si = math.cos(2 * math.pi * angle), sign * math.sin(2 * math.pi * angle)
    if angle in (0.125, 0.375):
        root = math.sqrt(0.5)
        if angle == 0.125:
            if sign > 0:
                return (re - im) * root, (re + im) * root
            return (re + im) * root, (im - re) * root
        if sign > 0:
            return (re + im) * (-root), (re - im) * root
        return (im - re) * root, (re + im) * (-root)
    return re * co - im * si, re * si + im * co


def add(a, b):
    return a[0] + b[0], a[1] + b[1]


def sub(a, b):
    return a[0] - b[0], a[1] - b[1]


def fft(values, sign):
    n = len(values)
    if n == 1:
        return values
    even, odd = fft(values[0::2], sign), fft(values[1::2], sign)
    out = [None] * n
    for k in range(n // 2):
        if k * 4 == n:
            re, im = odd[k]
            turned = (-im, re) if sign > 0 else (im, -re)
        else:
            turned = times(odd[k], k / n, sign)
        out[k] = add(even[k], turned)
        out[k + n // 2] = sub(even[k], turned)
    return out


def dot(a, b, dims):
    return lax.dot_general(a, b, (dims, ((), ())), preferred_element_type=F32)


def halves(value):
    high = value.astype(BF16)
    low = (value - high.astype(F32)).astype(BF16)
    return jnp.concatenate([high, low], axis=1)


def kernel(
    x_hbm, cot_hbm, w_hbm, table_hbm, tw_hbm, spread_hbm, first_hbm, gather_hbm, parity_hbm,
    out_ref, gw_ref,
    x_ref, cot_ref, w_ref, table, tw_ref, spread_ref, first_ref, gather_ref, parity_ref,
    send, recv, folded, even, weight, acc, spec, terms, mixed, dx, dg,
    load_sem, own_sem, send_sem, recv_sem, dp_send, dp_recv, dp_own,
):
    me = lax.axis_index("pencil")
    group = lax.axis_index("dp")
    stack, core = me // CORES, lax.rem(me, CORES)

    loads = [
        pltpu.make_async_copy(source, target, load_sem.at[place])
        for place, (source, target) in enumerate(
            [
                (x_hbm, x_ref),
                (table_hbm.at[0], table.at[0]),
                (table_hbm.at[1], table.at[1]),
                (parity_hbm, parity_ref),
                (w_hbm, w_ref),
                (tw_hbm, tw_ref),
                (spread_hbm, spread_ref),
                (gather_hbm, gather_ref),
                (first_hbm, first_ref),
                (cot_hbm, cot_ref),
            ]
        )
    ]
    for load in loads[:2]:
        load.start()

    barrier = pltpu.get_barrier_semaphore()

    def greet_pencil(i, carry):
        pl.semaphore_signal(
            barrier, inc=1, device_id=(group, lax.rem(me + i, PENCIL)), device_id_type=MESH
        )
        return carry

    def greet_group(i, carry):
        pl.semaphore_signal(
            barrier, inc=1, device_id=(lax.rem(group + i, GROUPS), me), device_id_type=MESH
        )
        return carry

    lax.fori_loop(1, PENCIL, greet_pencil, 0)
    lax.fori_loop(1, GROUPS, greet_group, 0)

    def block(ref, phase, parity, part, places):
        if part is None:
            return ref.at[phase, parity, places]
        return ref.at[phase, parity, places, part]

    def post(phase, parity, part, peer):
        slot = part or 0
        pltpu.make_async_remote_copy(
            src_ref=block(send, phase, parity, part, peer),
            dst_ref=block(recv, phase, parity, part, me),
            send_sem=send_sem.at[phase, parity, slot],
            recv_sem=recv_sem.at[phase, parity, slot],
            device_id=(group, peer),
            device_id_type=MESH,
        ).start()

    def own_copy(phase, parity, part):
        return pltpu.make_async_copy(
            block(send, phase, parity, part, me),
            block(recv, phase, parity, part, me),
            own_sem.at[phase, parity, part or 0],
        )

    def arrived(phase, parity, part):
        whole = block(recv, phase, parity, part, pl.ds(0, PENCIL - 1))
        pltpu.make_async_copy(whole, whole, recv_sem.at[phase, parity, part or 0]).wait()
        own_copy(phase, parity, part).wait()

    def sent(phase, parity, part):
        whole = block(send, phase, parity, part, pl.ds(0, PENCIL - 1))
        pltpu.make_async_copy(whole, whole, send_sem.at[phase, parity, part or 0]).wait()

    def stack_at(step):
        offset = STACKS // 2 + ((step + 1) // 2) * (2 * lax.rem(step, 2) - 1)
        return lax.rem(stack + offset + STACKS, STACKS)

    def post_stacks(phase, parity, part, steps):
        def one(i, carry):
            peer = stack_at(i // CORES) * CORES + lax.rem(core + i, CORES)

            @pl.when(peer != me)
            def _():
                post(phase, parity, part, peer)

            return carry

        lax.fori_loop(steps[0] * CORES, steps[1] * CORES, one, 0)

    def post_all(phase, parity, part):
        post_stacks(phase, parity, part, (0, STACKS))
        own_copy(phase, parity, part).start()

    lines_stack = CORES * 2 * DEEP

    def plane_forward(source, phase, parity, part, before_post=None):
        pieces = 2
        each = STACKS // pieces
        for piece in range(pieces):
            stacks = [stack_at(jnp.int32(piece * each + k)) for k in range(each)]
            lines = jnp.concatenate(
                [
                    table[parity, pl.ds(pl.multiple_of(at * lines_stack, lines_stack), lines_stack)]
                    for at in stacks
                ],
                axis=0,
            )
            result = dot(lines, source, ((1,), (1,))).astype(BF16)
            for k, at in enumerate(stacks):
                mine = result[k * lines_stack : (k + 1) * lines_stack]
                places = pl.ds(at * CORES, CORES)
                for place, half in enumerate((0, 1) if part is None else (part,)):
                    send[phase, parity, places, half] = mine[
                        :, place * HALF : (place + 1) * HALF
                    ].reshape(CORES, 2 * DEEP, HALF)
            if before_post is not None and piece == 0:
                before_post()
            post_stacks(phase, parity, part, (piece * each, (piece + 1) * each))
        own_copy(phase, parity, part).start()

    def first_forward(phase, parity, half):
        values = []
        for d in range(PENCIL):
            both = recv[phase, parity, d, half].astype(F32)
            values.append((both[:DEEP], both[DEEP:]))
        spectrum = fft(values, -1)
        for a in range(MX):
            re, im = spectrum[(a - MX // 2) % MX]
            co = tw_ref[a, 0:1, half * HALF : (half + 1) * HALF]
            si = tw_ref[a, 1:2, half * HALF : (half + 1) * HALF]
            for r, value in enumerate((re * co + im * si, im * co - re * si)):
                rows = slice(r * DEEP, (r + 1) * DEEP)
                acc[parity, a, rows] = value if half == 0 else acc[parity, a, rows] + value

    def first_inverse(phase, parity, half, scale):
        values = [None] * MX
        for a in range(MX):
            re, im = mixed[a, :DEEP], mixed[a, DEEP:]
            co = tw_ref[a, 0:1, half * HALF : (half + 1) * HALF]
            si = tw_ref[a, 1:2, half * HALF : (half + 1) * HALF]
            values[(a - MX // 2) % MX] = (re * co - im * si, im * co + re * si)
        signal = fft(values, 1)
        for d in range(PENCIL):
            both = jnp.concatenate(signal[d], axis=0)
            if scale is not None:
                both = both * scale
            send[phase, parity, d, half] = both.astype(BF16)

    mine_a = MX // GROUPS

    def share_own(source, target, which, parity):
        return pltpu.make_async_copy(
            source.at[parity, pl.ds(group * mine_a, mine_a)],
            target.at[parity, group],
            dp_own.at[which, parity],
        )

    def share(source, target, which, parity):
        def one(i, carry):
            peer = lax.rem(group + i, GROUPS)
            pltpu.make_async_remote_copy(
                src_ref=source.at[parity, pl.ds(peer * mine_a, mine_a)],
                dst_ref=target.at[parity, group],
                send_sem=dp_send.at[which, parity],
                recv_sem=dp_recv.at[which, parity],
                device_id=(peer, me),
                device_id_type=MESH,
            ).start()
            return carry

        lax.fori_loop(1, GROUPS, one, 0)
        share_own(source, target, which, parity).start()

    def shared(source, target, which, parity):
        whole = target.at[parity, pl.ds(0, GROUPS - 1)]
        pltpu.make_async_copy(whole, whole, dp_recv.at[which, parity]).wait()
        pltpu.make_async_copy(whole, whole, dp_send.at[which, parity]).wait()
        share_own(source, target, which, parity).wait()

    depth = lax.rem(lax.broadcasted_iota(jnp.int32, (2 * DEEP, HALF), 0), DEEP)
    volume = 1.0 / (NX * NY * NZ)
    scales = (
        jnp.where(depth == 0, volume, 2.0 * volume).astype(F32),
        jnp.full((2 * DEEP, HALF), 2.0 * volume, F32),
    )
    block_a = 8
    block_rows = block_a * 2 * DEEP
    lane_tiles = [slice(t * HALF, (t + 1) * HALF) for t in range(C * C // HALF)]

    def forward_mix(parity):
        def one(step, carry):
            own_a = pl.ds(step * block_a, block_a)
            lines = halves(acc[parity, own_a].reshape(block_rows, HALF))
            wide = dot(lines, spread_ref[...], ((1,), (0,)))
            spec[parity, own_a] = (
                wide[:, C * C :].astype(BF16).reshape(block_a, 2 * DEEP, HALF)
            )
            totals = []
            for a in range(block_a):
                out_re = jnp.zeros((DEEP, HALF), F32)
                out_im = jnp.zeros((DEEP, HALF), F32)
                row = a * 2 * DEEP
                for lanes in lane_tiles:
                    w_re = weight[parity, step * block_a + a, :DEEP, lanes]
                    w_im = weight[parity, step * block_a + a, DEEP:, lanes]
                    x_re = wide[row : row + DEEP, lanes]
                    x_im = wide[row + DEEP : row + 2 * DEEP, lanes]
                    out_re = out_re + x_re * w_re - x_im * w_im
                    out_im = out_im + x_re * w_im + x_im * w_re
                totals += [out_re, out_im]
            sums = dot(halves(jnp.concatenate(totals, axis=0)), spread_ref[:, C * C :], ((1,), (0,)))
            mixed[own_a] = sums.reshape(block_a, 2 * DEEP, HALF)
            return carry

        lax.fori_loop(0, MX // block_a, one, 0)

    def backward_mix(parity):
        def one(step, carry):
            own_a = pl.ds(step * block_a, block_a)
            lines = halves(acc[parity, own_a].reshape(block_rows, HALF))
            sums = dot(lines, spread_ref[:, C * C :], ((1,), (0,)))
            narrow = (sums.reshape(block_a, 2 * DEEP, HALF) * scales[parity]).astype(BF16)
            terms[parity, own_a] = narrow
            grads = narrow.astype(F32)
            products = []
            for a in range(block_a):
                g_re, g_im = grads[a, :DEEP], grads[a, DEEP:]
                tiles = []
                for lanes in lane_tiles:
                    w_re = weight[parity, step * block_a + a, :DEEP, lanes]
                    w_im = weight[parity, step * block_a + a, DEEP:, lanes]
                    tiles.append(
                        jnp.concatenate(
                            [g_re * w_re + g_im * w_im, g_im * w_re - g_re * w_im], axis=0
                        ).astype(BF16)
                    )
                products.append(jnp.concatenate(tiles, axis=1))
            result = dot(jnp.concatenate(products, axis=0), gather_ref[...], ((1,), (0,)))
            mixed[own_a] = result.reshape(block_a, 2 * DEEP, HALF)
            return carry

        lax.fori_loop(0, MX // block_a, one, 0)

    width = 512

    def lines_of(phase, parity, half):
        return recv[phase, parity, :, half].reshape(SPEC // 2, HALF)

    def even_cells(phase):
        lines = jnp.concatenate([lines_of(phase, 0, 0), lines_of(phase, 0, 1)], axis=1).T

        def one(step, carry):
            lanes = pl.ds(pl.multiple_of(step * width, width), width)
            even[:, lanes] = dot(lines, table[0, :, lanes], ((1,), (0,)))
            return carry

        lax.fori_loop(0, FOLD // width, one, 0)

    def odd_cells(phase, half, finish):
        lines = lines_of(phase, 1, half).T
        rows = pl.ds(half * HALF, HALF)

        def one(step, carry):
            near = pl.ds(pl.multiple_of(step * width, width), width)
            far = pl.ds(pl.multiple_of(FOLD + step * width, width), width)
            odd = dot(lines, table[1, :, near], ((1,), (0,)))
            base = even[rows, near]
            finish(rows, near, far, base + odd, base - odd)
            return carry

        lax.fori_loop(0, FOLD // width, one, 0, unroll=True)

    loads[0].wait()
    for load in loads[2:]:
        load.start()

    def fold_fields(step, carry):
        near = pl.ds(pl.multiple_of(step * width, width), width)
        far = pl.ds(pl.multiple_of(FOLD + step * width, width), width)
        one, two = x_ref[:, near], x_ref[:, far]
        folded[0, :, near] = one + two
        folded[1, :, near] = one - two
        return carry

    lax.fori_loop(0, FOLD // width, fold_fields, 0)
    loads[1].wait()

    def all_here():
        pl.semaphore_wait(barrier, PENCIL + GROUPS - 2)

    plane_forward(folded[0], 0, 0, None, all_here)
    loads[2].wait()
    plane_forward(folded[1], 0, 1, None)

    loads[3].wait()
    loads[4].wait()

    def part_weights(step, carry):
        own_a = pl.ds(step * 4, 4)
        lines = w_ref[own_a].reshape(HALF, C * C)
        apart = dot(parity_ref[...], lines, ((1,), (0,)))
        for parity in range(2):
            weight[parity, own_a] = apart[parity * HALF // 2 : (parity + 1) * HALF // 2].reshape(
                4, 2 * DEEP, C * C
            )
        return carry

    lax.fori_loop(0, MX // 4, part_weights, 0)
    for load in loads[5:]:
        load.wait()

    for parity in range(2):
        arrived(0, parity, None)
        for half in range(2):
            first_forward(0, parity, half)
        forward_mix(parity)
        share(spec, dx, 0, parity)
        for half in range(2):
            first_inverse(1, parity, half, scales[parity])
            if parity == 1:
                post_all(1, parity, half)
        if parity == 0:
            post_all(1, parity, None)

    arrived(1, 0, None)
    even_cells(1)

    def slopes(rows, near, far, one, two):
        one = gelu_slope(one) * cot_ref[rows, near].astype(F32)
        two = gelu_slope(two) * cot_ref[rows, far].astype(F32)
        folded[0, rows, near] = (one + two).astype(BF16)
        folded[1, rows, near] = (one - two).astype(BF16)

    for half in range(2):
        arrived(1, 1, half)
        odd_cells(1, half, slopes)
        for parity in range(2):
            plane_forward(folded[parity, pl.ds(half * HALF, HALF)], 2, parity, half)

    for parity in range(2):
        arrived(2, parity, 0)
        first_forward(2, parity, 0)
    for parity in range(2):
        arrived(2, parity, 1)
        first_forward(2, parity, 1)
        backward_mix(parity)
        share(terms, dg, 1, parity)
        for half in range(2):
            first_inverse(3, parity, half, None)
            if parity == 1:
                post_all(3, parity, half)
        if parity == 0:
            post_all(3, parity, None)

    for parity in range(2):
        shared(spec, dx, 0, parity)
        shared(terms, dg, 1, parity)

    def outer(a, carry):
        for parity in range(2):
            lines = dx[parity, :, a].reshape(HALF, HALF)
            wide = dot(lines, first_ref[...], ((1,), (0,)))
            factors = [dg[parity, s, a].astype(F32) for s in range(GROUPS)]
            for tile, lanes in enumerate(lane_tiles):
                out_re = jnp.zeros((DEEP, HALF), F32)
                out_im = jnp.zeros((DEEP, HALF), F32)
                for s in range(GROUPS):
                    row = s * 2 * DEEP
                    x_re, x_im = wide[row : row + DEEP, lanes], wide[row + DEEP : row + 2 * DEEP, lanes]
                    g_re, g_im = factors[s][:DEEP], factors[s][DEEP:]
                    out_re = out_re + x_re * g_re + x_im * g_im
                    out_im = out_im + x_re * g_im - x_im * g_re
                gw_ref[tile, a, 0, pl.ds(parity, DEEP, stride=2)] = out_re
                gw_ref[tile, a, 1, pl.ds(parity, DEEP, stride=2)] = out_im
        return carry

    lax.fori_loop(0, MX // GROUPS, outer, 0)
    arrived(3, 0, None)
    even_cells(3)

    def finish(rows, near, far, one, two):
        out_ref[rows, near] = one.astype(BF16)
        out_ref[rows, far] = two.astype(BF16)

    for half in range(2):
        arrived(3, 1, half)
        odd_cells(3, half, finish)

    for parity in range(2):
        sent(0, parity, None)
        for half in range(2):
            sent(2, parity, half)
    for phase in (1, 3):
        sent(phase, 0, None)
        for half in range(2):
            sent(phase, 1, half)


def store_kernel(out_ref, gw_ref, out_hbm, gw_hbm, sems):
    copies = []
    for place in range(STORES):
        rows = pl.ds(place * (ROWS // STORES), ROWS // STORES)
        copies.append(pltpu.make_async_copy(out_ref.at[rows], out_hbm.at[rows], sems.at[place]))
    for tile in range(C * C // HALF):
        lanes = slice(tile * HALF, (tile + 1) * HALF)
        copies.append(
            pltpu.make_async_copy(
                gw_ref.at[tile], gw_hbm.at[:, :, :, lanes], sems.at[STORES + tile]
            )
        )
    for copy in copies:
        copy.start()
    for copy in copies:
        copy.wait()


def per_device(fields, cotangent, spectral_weight):
    any_space = pl.BlockSpec(memory_space=pl.ANY)
    vmem = pl.BlockSpec(memory_space=pltpu.VMEM)
    messages = (4, 2, PENCIL, 2, 2 * DEEP, HALF)
    spectrum = (2, MX, 2 * DEEP, HALF)
    mine = MX // GROUPS
    constants = [jnp.asarray(table) for table in tables()]
    grad_fields, grad_weight = pl.pallas_call(
        kernel,
        out_shape=(
            pltpu.VMEM((ROWS, PLANE), BF16),
            pltpu.VMEM((C * C // HALF, mine, 2, MZ, HALF), F32),
        ),
        in_specs=[any_space] * (3 + len(constants)),
        out_specs=(vmem, vmem),
        scratch_shapes=[
            pltpu.VMEM((ROWS, PLANE), BF16),
            pltpu.VMEM((ROWS, PLANE), BF16),
            pltpu.VMEM((MX, 2, MZ, C * C), BF16),
        ]
        + [pltpu.VMEM(table.shape, table.dtype) for table in constants]
        + [
            pltpu.VMEM(messages, BF16),
            pltpu.VMEM(messages, BF16),
            pltpu.VMEM((2, ROWS, FOLD), BF16),
            pltpu.VMEM((ROWS, FOLD), F32),
            pltpu.VMEM((2, MX, 2 * DEEP, C * C), F32),
            pltpu.VMEM((2, MX, 2 * DEEP, HALF), F32),
            pltpu.VMEM(spectrum, BF16),
            pltpu.VMEM(spectrum, BF16),
            pltpu.VMEM((MX, 2 * DEEP, HALF), F32),
            pltpu.VMEM((2, GROUPS, mine, 2 * DEEP, HALF), BF16),
            pltpu.VMEM((2, GROUPS, mine, 2 * DEEP, HALF), BF16),
            pltpu.SemaphoreType.DMA((10,)),
            pltpu.SemaphoreType.DMA((4, 2, 2)),
            pltpu.SemaphoreType.DMA((4, 2, 2)),
            pltpu.SemaphoreType.DMA((4, 2, 2)),
            pltpu.SemaphoreType.DMA((2, 2)),
            pltpu.SemaphoreType.DMA((2, 2)),
            pltpu.SemaphoreType.DMA((2, 2)),
        ],
        compiler_params=pltpu.CompilerParams(
            collective_id=0, has_side_effects=True, vmem_limit_bytes=56 * 2**20
        ),
        cost_estimate=pl.CostEstimate(
            flops=5 * 10**9, bytes_accessed=16 * 2**20, transcendentals=2**21
        ),
    )(
        *(
            pltpu.with_memory_space_constraint(operand, pltpu.HBM)
            for operand in (
                fields.reshape(ROWS, PLANE),
                cotangent.reshape(ROWS, PLANE),
                spectral_weight,
                *constants,
            )
        )
    )
    grad_fields, grad_weight = pl.pallas_call(
        store_kernel,
        out_shape=(
            jax.ShapeDtypeStruct((ROWS, PLANE), BF16),
            jax.ShapeDtypeStruct((mine, 2, MZ, C * C), F32),
        ),
        in_specs=[vmem, vmem],
        out_specs=(any_space, any_space),
        scratch_shapes=[pltpu.SemaphoreType.DMA((STORES + C * C // HALF,))],
        compiler_params=pltpu.CompilerParams(vmem_limit_bytes=2 * 2**20),
    )(
        pltpu.with_memory_space_constraint(grad_fields, pltpu.VMEM),
        pltpu.with_memory_space_constraint(grad_weight, pltpu.VMEM),
    )
    return grad_fields.reshape(1, XD, C, PLANE), grad_weight


def solution(mesh):
    placed = (
        P("dp", "pencil", None, None),
        P("dp", "pencil", None, None),
        P(None, None, "pencil", None),
    )
    return jax.shard_map(
        per_device,
        mesh=mesh,
        in_specs=placed,
        out_specs=(P("dp", "pencil", None, None), P("dp", None, "pencil", None)),
        check_vma=False,
    )
```

```python
import functools
import math

import jax
import jax.numpy as jnp
import numpy as np
from jax import lax
from jax.experimental import pallas as pl
from jax.experimental.pallas import tpu as pltpu
from jax.sharding import PartitionSpec as P

C = 32
MX = 32
MY = 32
MZ = 16
NX = 256
NY = 128
NZ = 32
PLANE = NY * NZ
PENCIL = 32
GROUPS = 8
XD = NX // PENCIL
ROWS = XD * C
SPEC = PENCIL * 2 * MZ
HALF = 128
FOLD = PLANE // 2
DEEP = MZ // 2
STORES = 8
STACKS = 8
CORES = PENCIL // STACKS
MESH = pl.DeviceIdType.MESH
F32 = jnp.float32
BF16 = jnp.bfloat16

ROOT_HALF = 0.7071067811865476
DENSITY = 0.3989422804014327


def gelu_slope(v):
    return 0.5 * (1.0 + lax.erf(v * ROOT_HALF)) + v * jnp.exp(-0.5 * v * v) * DENSITY


@functools.lru_cache(None)
def tables():
    b = np.arange(MY)[None, :, None, None]
    c = 2 * np.arange(DEEP)[None, None, :, None] + np.arange(2)[:, None, None, None]
    p = np.arange(FOLD)[None, None, None, :]
    y, z = p % NY, p // NY
    turns = ((b - MY // 2) * y * NZ + c * z * NY) % PLANE
    angle = turns * (2.0 * math.pi / PLANE)
    plane = np.stack([np.cos(angle), -np.sin(angle)], axis=2).reshape(2, SPEC // 2, FOLD)
    kx = np.arange(MX)[:, None] - MX // 2
    j = np.arange(ROWS)[None, :] // C
    phase = ((kx * j) % NX) * (2.0 * math.pi / NX)
    twiddle = np.stack([np.cos(phase), np.sin(phase)], axis=1)
    lane = np.arange(HALF)
    pairs = np.arange(C * C)
    wide = (lane[:, None] % C) == (pairs[None, :] // C)
    again = (lane[:, None] % C) == (lane[None, :] % C)
    spread = np.tile(np.concatenate([wide, again], axis=1), (2, 1))
    first = wide * (lane[:, None] < C)
    gather = (pairs[:, None] // C) == (lane[None, :] % C)
    order = np.arange(HALF).reshape(4, 2, DEEP, 2).transpose(3, 0, 1, 2).reshape(-1)
    parity = np.zeros((HALF, HALF))
    parity[np.arange(HALF), order] = 1.0
    return (
        plane.astype(jnp.bfloat16),
        twiddle.astype(np.float32),
        spread.astype(jnp.bfloat16),
        first.astype(jnp.bfloat16),
        gather.astype(jnp.bfloat16),
        parity.astype(jnp.bfloat16),
    )


def times(value, angle, sign):
    re, im = value
    if angle == 0:
        return value
    co, si = math.cos(2 * math.pi * angle), sign * math.sin(2 * math.pi * angle)
    if angle in (0.125, 0.375):
        root = math.sqrt(0.5)
        if angle == 0.125:
            if sign > 0:
                return (re - im) * root, (re + im) * root
            return (re + im) * root, (im - re) * root
        if sign > 0:
            return (re + im) * (-root), (re - im) * root
        return (im - re) * root, (re + im) * (-root)
    return re * co - im * si, re * si + im * co


def add(a, b):
    return a[0] + b[0], a[1] + b[1]


def sub(a, b):
    return a[0] - b[0], a[1] - b[1]


def fft(values, sign):
    n = len(values)
    if n == 1:
        return values
    even, odd = fft(values[0::2], sign), fft(values[1::2], sign)
    out = [None] * n
    for k in range(n // 2):
        if k * 4 == n:
            re, im = odd[k]
            turned = (-im, re) if sign > 0 else (im, -re)
        else:
            turned = times(odd[k], k / n, sign)
        out[k] = add(even[k], turned)
        out[k + n // 2] = sub(even[k], turned)
    return out


def dot(a, b, dims):
    return lax.dot_general(a, b, (dims, ((), ())), preferred_element_type=F32)


def halves(value):
    high = value.astype(BF16)
    low = (value - high.astype(F32)).astype(BF16)
    return jnp.concatenate([high, low], axis=1)


def kernel(
    x_hbm, cot_hbm, w_hbm, table_hbm, tw_hbm, spread_hbm, first_hbm, gather_hbm, parity_hbm,
    out_ref, gw_ref, odd_table, even, tail_ref,
    x_ref, cot_ref, w_ref, even_table, tw_ref, spread_ref, first_ref, gather_ref, parity_ref,
    send, recv, folded, weight, acc, spec, terms, mixed, dx, dg,
    x_sem, table_sem, load_sem, own_sem, send_sem, recv_sem, dp_send, dp_recv, dp_own,
):
    table = (even_table, odd_table)
    me = lax.axis_index("pencil")
    group = lax.axis_index("dp")
    stack, core = me // CORES, lax.rem(me, CORES)

    width = 512
    blocks = FOLD // width
    lines_stack = CORES * 2 * DEEP

    def stack_at(step):
        offset = STACKS // 2 + ((step + 1) // 2) * (2 * lax.rem(step, 2) - 1)
        return lax.rem(stack + offset + STACKS, STACKS)

    def stack_lines(step):
        return pl.ds(pl.multiple_of(stack_at(jnp.int32(step)) * lines_stack, lines_stack), lines_stack)

    load_x = []
    for step in range(blocks):
        for far in range(2):
            lanes = pl.ds(far * FOLD + step * width, width)
            load_x.append(
                pltpu.make_async_copy(x_hbm.at[:, lanes], x_ref.at[:, lanes], x_sem.at[step, far])
            )
    load_table = [
        pltpu.make_async_copy(
            table_hbm.at[0, stack_lines(step)], even_table.at[stack_lines(step)], table_sem.at[step]
        )
        for step in range(STACKS)
    ]
    loads = [
        pltpu.make_async_copy(source, target, load_sem.at[place])
        for place, (source, target) in enumerate(
            [
                (table_hbm.at[1], odd_table),
                (parity_hbm, parity_ref),
                (w_hbm, w_ref),
                (tw_hbm, tw_ref),
                (spread_hbm, spread_ref),
                (gather_hbm, gather_ref),
                (first_hbm, first_ref),
                (cot_hbm, cot_ref),
            ]
        )
    ]
    for load in load_x + load_table:
        load.start()

    barrier = pltpu.get_barrier_semaphore()

    def greet_pencil(i, carry):
        pl.semaphore_signal(
            barrier, inc=1, device_id=(group, lax.rem(me + i, PENCIL)), device_id_type=MESH
        )
        return carry

    def greet_group(i, carry):
        pl.semaphore_signal(
            barrier, inc=1, device_id=(lax.rem(group + i, GROUPS), me), device_id_type=MESH
        )
        return carry

    lax.fori_loop(1, PENCIL, greet_pencil, 0)
    lax.fori_loop(1, GROUPS, greet_group, 0)

    def block(ref, phase, parity, part, places):
        if part is None:
            return ref.at[phase, parity, places]
        return ref.at[phase, parity, places, part]

    def post(phase, parity, part, peer):
        slot = part or 0
        pltpu.make_async_remote_copy(
            src_ref=block(send, phase, parity, part, peer),
            dst_ref=block(recv, phase, parity, part, me),
            send_sem=send_sem.at[phase, parity, slot],
            recv_sem=recv_sem.at[phase, parity, slot],
            device_id=(group, peer),
            device_id_type=MESH,
        ).start()

    def own_copy(phase, parity, part):
        return pltpu.make_async_copy(
            block(send, phase, parity, part, me),
            block(recv, phase, parity, part, me),
            own_sem.at[phase, parity, part or 0],
        )

    def arrived(phase, parity, part):
        whole = block(recv, phase, parity, part, pl.ds(0, PENCIL - 1))
        pltpu.make_async_copy(whole, whole, recv_sem.at[phase, parity, part or 0]).wait()
        own_copy(phase, parity, part).wait()

    def sent(phase, parity, part):
        whole = block(send, phase, parity, part, pl.ds(0, PENCIL - 1))
        pltpu.make_async_copy(whole, whole, send_sem.at[phase, parity, part or 0]).wait()

    def post_stacks(phase, parity, part, steps):
        def one(i, carry):
            peer = stack_at(i // CORES) * CORES + lax.rem(core + i, CORES)

            @pl.when(peer != me)
            def _():
                post(phase, parity, part, peer)

            return carry

        lax.fori_loop(steps[0] * CORES, steps[1] * CORES, one, 0)

    def post_all(phase, parity, part):
        post_stacks(phase, parity, part, (0, STACKS))
        own_copy(phase, parity, part).start()

    def plane_forward(source, phase, parity, part, ready=None, before_post=None):
        pieces = 2
        each = STACKS // pieces
        for piece in range(pieces):
            steps = range(piece * each, (piece + 1) * each)
            if ready is not None:
                for step in steps:
                    ready[step].wait()
            lines = jnp.concatenate([table[parity][stack_lines(step)] for step in steps], axis=0)
            result = dot(lines, source, ((1,), (1,))).astype(BF16)
            for k, step in enumerate(steps):
                mine = result[k * lines_stack : (k + 1) * lines_stack]
                places = pl.ds(stack_at(jnp.int32(step)) * CORES, CORES)
                for place, half in enumerate((0, 1) if part is None else (part,)):
                    send[phase, parity, places, half] = mine[
                        :, place * HALF : (place + 1) * HALF
                    ].reshape(CORES, 2 * DEEP, HALF)
            if before_post is not None and piece == 0:
                before_post()
            post_stacks(phase, parity, part, (piece * each, (piece + 1) * each))
        own_copy(phase, parity, part).start()

    def first_forward(phase, parity, half):
        values = []
        for d in range(PENCIL):
            both = recv[phase, parity, d, half].astype(F32)
            values.append((both[:DEEP], both[DEEP:]))
        spectrum = fft(values, -1)
        for a in range(MX):
            re, im = spectrum[(a - MX // 2) % MX]
            co = tw_ref[a, 0:1, half * HALF : (half + 1) * HALF]
            si = tw_ref[a, 1:2, half * HALF : (half + 1) * HALF]
            for r, value in enumerate((re * co + im * si, im * co - re * si)):
                rows = slice(r * DEEP, (r + 1) * DEEP)
                acc[parity, a, rows] = value if half == 0 else acc[parity, a, rows] + value

    def first_inverse(phase, parity, half, scale):
        values = [None] * MX
        for a in range(MX):
            re, im = mixed[a, :DEEP], mixed[a, DEEP:]
            co = tw_ref[a, 0:1, half * HALF : (half + 1) * HALF]
            si = tw_ref[a, 1:2, half * HALF : (half + 1) * HALF]
            values[(a - MX // 2) % MX] = (re * co - im * si, im * co + re * si)
        signal = fft(values, 1)
        for d in range(PENCIL):
            both = jnp.concatenate(signal[d], axis=0)
            if scale is not None:
                both = both * scale
            send[phase, parity, d, half] = both.astype(BF16)

    mine_a = MX // GROUPS

    def share_own(source, target, which, parity):
        return pltpu.make_async_copy(
            source.at[parity, pl.ds(group * mine_a, mine_a)],
            target.at[parity, group],
            dp_own.at[which, parity],
        )

    def share(source, target, which, parity):
        def one(i, carry):
            peer = lax.rem(group + i, GROUPS)
            pltpu.make_async_remote_copy(
                src_ref=source.at[parity, pl.ds(peer * mine_a, mine_a)],
                dst_ref=target.at[parity, group],
                send_sem=dp_send.at[which, parity],
                recv_sem=dp_recv.at[which, parity],
                device_id=(peer, me),
                device_id_type=MESH,
            ).start()
            return carry

        lax.fori_loop(1, GROUPS, one, 0)
        share_own(source, target, which, parity).start()

    def shared(source, target, which, parity):
        whole = target.at[parity, pl.ds(0, GROUPS - 1)]
        pltpu.make_async_copy(whole, whole, dp_recv.at[which, parity]).wait()
        pltpu.make_async_copy(whole, whole, dp_send.at[which, parity]).wait()
        share_own(source, target, which, parity).wait()

    depth = lax.rem(lax.broadcasted_iota(jnp.int32, (2 * DEEP, HALF), 0), DEEP)
    volume = 1.0 / (NX * NY * NZ)
    scales = (
        jnp.where(depth == 0, volume, 2.0 * volume).astype(F32),
        jnp.full((2 * DEEP, HALF), 2.0 * volume, F32),
    )
    block_a = 8
    block_rows = block_a * 2 * DEEP
    lane_tiles = [slice(t * HALF, (t + 1) * HALF) for t in range(C * C // HALF)]

    def forward_mix(parity):
        def one(step, carry):
            own_a = pl.ds(step * block_a, block_a)
            lines = halves(acc[parity, own_a].reshape(block_rows, HALF))
            wide = dot(lines, spread_ref[...], ((1,), (0,)))
            spec[parity, own_a] = (
                wide[:, C * C :].astype(BF16).reshape(block_a, 2 * DEEP, HALF)
            )
            totals = []
            for a in range(block_a):
                out_re = jnp.zeros((DEEP, HALF), F32)
                out_im = jnp.zeros((DEEP, HALF), F32)
                row = a * 2 * DEEP
                for lanes in lane_tiles:
                    w_re = weight[parity, step * block_a + a, :DEEP, lanes]
                    w_im = weight[parity, step * block_a + a, DEEP:, lanes]
                    x_re = wide[row : row + DEEP, lanes]
                    x_im = wide[row + DEEP : row + 2 * DEEP, lanes]
                    out_re = out_re + x_re * w_re - x_im * w_im
                    out_im = out_im + x_re * w_im + x_im * w_re
                totals += [out_re, out_im]
            sums = dot(halves(jnp.concatenate(totals, axis=0)), spread_ref[:, C * C :], ((1,), (0,)))
            mixed[own_a] = sums.reshape(block_a, 2 * DEEP, HALF)
            return carry

        lax.fori_loop(0, MX // block_a, one, 0, unroll=2)

    def backward_mix(parity):
        def one(step, carry):
            own_a = pl.ds(step * block_a, block_a)
            lines = halves(acc[parity, own_a].reshape(block_rows, HALF))
            sums = dot(lines, spread_ref[:, C * C :], ((1,), (0,)))
            narrow = (sums.reshape(block_a, 2 * DEEP, HALF) * scales[parity]).astype(BF16)
            terms[parity, own_a] = narrow
            grads = narrow.astype(F32)
            products = []
            for a in range(block_a):
                g_re, g_im = grads[a, :DEEP], grads[a, DEEP:]
                tiles = []
                for lanes in lane_tiles:
                    w_re = weight[parity, step * block_a + a, :DEEP, lanes]
                    w_im = weight[parity, step * block_a + a, DEEP:, lanes]
                    tiles.append(
                        jnp.concatenate(
                            [g_re * w_re + g_im * w_im, g_im * w_re - g_re * w_im], axis=0
                        ).astype(BF16)
                    )
                products.append(jnp.concatenate(tiles, axis=1))
            result = dot(jnp.concatenate(products, axis=0), gather_ref[...], ((1,), (0,)))
            mixed[own_a] = result.reshape(block_a, 2 * DEEP, HALF)
            return carry

        lax.fori_loop(0, MX // block_a, one, 0, unroll=2)

    def lines_of(phase, parity, half):
        return recv[phase, parity, :, half].reshape(SPEC // 2, HALF)

    def even_cells(phase, half):
        if half is None:
            lines = jnp.concatenate([lines_of(phase, 0, 0), lines_of(phase, 0, 1)], axis=1).T
            rows = pl.ds(0, ROWS)
        else:
            lines = lines_of(phase, 0, half).T
            rows = pl.ds(half * HALF, HALF)

        def one(step, carry):
            lanes = pl.ds(pl.multiple_of(step * width, width), width)
            even[rows, lanes] = dot(lines, even_table[:, lanes], ((1,), (0,)))
            return carry

        lax.fori_loop(0, FOLD // width, one, 0)

    def odd_cells(phase, half, finish):
        lines = lines_of(phase, 1, half).T
        rows = pl.ds(half * HALF, HALF)

        def one(step, carry):
            near = pl.ds(pl.multiple_of(step * width, width), width)
            far = pl.ds(pl.multiple_of(FOLD + step * width, width), width)
            odd = dot(lines, odd_table[:, near], ((1,), (0,)))
            base = even[rows, near]
            finish(rows, near, far, base + odd, base - odd)
            return carry

        lax.fori_loop(0, FOLD // width, one, 0, unroll=True)

    for step in range(blocks):
        near, far = pl.ds(step * width, width), pl.ds(FOLD + step * width, width)
        load_x[2 * step].wait()
        load_x[2 * step + 1].wait()
        one, two = x_ref[:, near], x_ref[:, far]
        folded[0, :, near] = one + two
        folded[1, :, near] = one - two
    for load in loads:
        load.start()

    def all_here():
        pl.semaphore_wait(barrier, PENCIL + GROUPS - 2)

    plane_forward(folded[0], 0, 0, None, load_table, all_here)
    loads[0].wait()
    plane_forward(folded[1], 0, 1, None)

    loads[1].wait()
    loads[2].wait()

    def part_weights(step, carry):
        own_a = pl.ds(step * 4, 4)
        lines = w_ref[own_a].reshape(HALF, C * C)
        apart = dot(parity_ref[...], lines, ((1,), (0,)))
        for parity in range(2):
            weight[parity, own_a] = apart[parity * HALF // 2 : (parity + 1) * HALF // 2].reshape(
                4, 2 * DEEP, C * C
            )
        return carry

    lax.fori_loop(0, MX // 4, part_weights, 0)
    for load in loads[3:]:
        load.wait()

    for parity in range(2):
        arrived(0, parity, None)
        for half in range(2):
            first_forward(0, parity, half)
        forward_mix(parity)
        for half in range(2):
            first_inverse(1, parity, half, scales[parity])
            if half == 0:
                post_all(1, parity, 0)
    for parity in range(2):
        post_all(1, parity, 1)


    def slopes(rows, near, far, one, two):
        one = gelu_slope(one) * cot_ref[rows, near].astype(F32)
        two = gelu_slope(two) * cot_ref[rows, far].astype(F32)
        folded[0, rows, near] = (one + two).astype(BF16)
        folded[1, rows, near] = (one - two).astype(BF16)

    for half in range(2):
        arrived(1, 0, half)
        even_cells(1, half)
        arrived(1, 1, half)
        odd_cells(1, half, slopes)
        for parity in range(2):
            plane_forward(folded[parity, pl.ds(half * HALF, HALF)], 2, parity, half)
    for parity in range(2):
        share(spec, dx, 0, parity)

    for parity in range(2):
        arrived(2, parity, 0)
        first_forward(2, parity, 0)
    for parity in range(2):
        arrived(2, parity, 1)
        first_forward(2, parity, 1)
        backward_mix(parity)
        share(terms, dg, 1, parity)
        for half in range(2):
            first_inverse(3, parity, half, None)
            if parity == 1:
                post_all(3, parity, half)
        if parity == 0:
            post_all(3, parity, None)

    for parity in range(2):
        shared(spec, dx, 0, parity)
        shared(terms, dg, 1, parity)

    def outer(a, carry):
        for parity in range(2):
            lines = dx[parity, :, a].reshape(HALF, HALF)
            wide = dot(lines, first_ref[...], ((1,), (0,)))
            factors = [dg[parity, s, a].astype(F32) for s in range(GROUPS)]
            for tile, lanes in enumerate(lane_tiles):
                out_re = jnp.zeros((DEEP, HALF), F32)
                out_im = jnp.zeros((DEEP, HALF), F32)
                for s in range(GROUPS):
                    row = s * 2 * DEEP
                    x_re, x_im = wide[row : row + DEEP, lanes], wide[row + DEEP : row + 2 * DEEP, lanes]
                    g_re, g_im = factors[s][:DEEP], factors[s][DEEP:]
                    out_re = out_re + x_re * g_re + x_im * g_im
                    out_im = out_im + x_re * g_im - x_im * g_re
                gw_ref[tile, a, 0, pl.ds(parity, DEEP, stride=2)] = out_re
                gw_ref[tile, a, 1, pl.ds(parity, DEEP, stride=2)] = out_im
        return carry

    lax.fori_loop(0, MX // GROUPS, outer, 0, unroll=2)
    arrived(3, 0, None)
    even_cells(3, None)

    def finish(rows, near, far, one, two):
        out_ref[rows, near] = one.astype(BF16)
        out_ref[rows, far] = two.astype(BF16)

    arrived(3, 1, 0)
    odd_cells(3, 0, finish)
    arrived(3, 1, 1)
    tail_ref[...] = lines_of(3, 1, 1).T

    for parity in range(2):
        sent(0, parity, None)
        for half in range(2):
            sent(2, parity, half)
        for half in range(2):
            sent(1, parity, half)
    sent(3, 0, None)
    for half in range(2):
        sent(3, 1, half)


def last_kernel(
    out_ref, gw_ref, table_ref, even_ref, lines_ref, out_hbm, gw_hbm, tail, store_sem, tail_sem
):
    stores = []
    for place in range(STORES):
        rows = pl.ds(place * (HALF // STORES), HALF // STORES)
        stores.append(
            pltpu.make_async_copy(out_ref.at[rows], out_hbm.at[rows], store_sem.at[place])
        )
    for tile in range(C * C // HALF):
        lanes = slice(tile * HALF, (tile + 1) * HALF)
        stores.append(
            pltpu.make_async_copy(
                gw_ref.at[tile], gw_hbm.at[:, :, :, lanes], store_sem.at[STORES + tile]
            )
        )
    for store in stores:
        store.start()
    width = 512
    rows = pl.ds(HALF, HALF)
    for step in range(FOLD // width):
        near, far = pl.ds(step * width, width), pl.ds(FOLD + step * width, width)
        odd = dot(lines_ref[...], table_ref[:, near], ((1,), (0,)))
        base = even_ref[rows, near]
        tail[:, near] = (base + odd).astype(BF16)
        tail[:, far] = (base - odd).astype(BF16)
        for place, lanes in enumerate((near, far)):
            store = pltpu.make_async_copy(
                tail.at[:, lanes], out_hbm.at[rows, lanes], tail_sem.at[step, place]
            )
            store.start()
            stores.append(store)
    for store in stores:
        store.wait()


def per_device(fields, cotangent, spectral_weight):
    any_space = pl.BlockSpec(memory_space=pl.ANY)
    vmem = pl.BlockSpec(memory_space=pltpu.VMEM)
    messages = (4, 2, PENCIL, 2, 2 * DEEP, HALF)
    spectrum = (2, MX, 2 * DEEP, HALF)
    mine = MX // GROUPS
    constants = [jnp.asarray(table) for table in tables()]
    results = pl.pallas_call(
        kernel,
        out_shape=(
            pltpu.VMEM((HALF, PLANE), BF16),
            pltpu.VMEM((C * C // HALF, mine, 2, MZ, HALF), F32),
            pltpu.VMEM((SPEC // 2, FOLD), BF16),
            pltpu.VMEM((ROWS, FOLD), F32),
            pltpu.VMEM((HALF, SPEC // 2), BF16),
        ),
        in_specs=[any_space] * (3 + len(constants)),
        out_specs=(vmem,) * 5,
        scratch_shapes=[
            pltpu.VMEM((ROWS, PLANE), BF16),
            pltpu.VMEM((ROWS, PLANE), BF16),
            pltpu.VMEM((MX, 2, MZ, C * C), BF16),
        ]
        + [pltpu.VMEM(constants[0].shape[1:], BF16)]
        + [pltpu.VMEM(table.shape, table.dtype) for table in constants[1:]]
        + [
            pltpu.VMEM(messages, BF16),
            pltpu.VMEM(messages, BF16),
            pltpu.VMEM((2, ROWS, FOLD), BF16),
            pltpu.VMEM((2, MX, 2 * DEEP, C * C), F32),
            pltpu.VMEM((2, MX, 2 * DEEP, HALF), F32),
            pltpu.VMEM(spectrum, BF16),
            pltpu.VMEM(spectrum, BF16),
            pltpu.VMEM((MX, 2 * DEEP, HALF), F32),
            pltpu.VMEM((2, GROUPS, mine, 2 * DEEP, HALF), BF16),
            pltpu.VMEM((2, GROUPS, mine, 2 * DEEP, HALF), BF16),
            pltpu.SemaphoreType.DMA((4, 2)),
            pltpu.SemaphoreType.DMA((STACKS,)),
            pltpu.SemaphoreType.DMA((8,)),
            pltpu.SemaphoreType.DMA((4, 2, 2)),
            pltpu.SemaphoreType.DMA((4, 2, 2)),
            pltpu.SemaphoreType.DMA((4, 2, 2)),
            pltpu.SemaphoreType.DMA((2, 2)),
            pltpu.SemaphoreType.DMA((2, 2)),
            pltpu.SemaphoreType.DMA((2, 2)),
        ],
        compiler_params=pltpu.CompilerParams(
            collective_id=0, has_side_effects=True, vmem_limit_bytes=48 * 2**20
        ),
        cost_estimate=pl.CostEstimate(
            flops=5 * 10**9, bytes_accessed=16 * 2**20, transcendentals=2**21
        ),
    )(
        *(
            pltpu.with_memory_space_constraint(operand, pltpu.HBM)
            for operand in (
                fields.reshape(ROWS, PLANE),
                cotangent.reshape(ROWS, PLANE),
                spectral_weight,
                *constants,
            )
        )
    )
    grad_fields, grad_weight = pl.pallas_call(
        last_kernel,
        out_shape=(
            jax.ShapeDtypeStruct((ROWS, PLANE), BF16),
            jax.ShapeDtypeStruct((mine, 2, MZ, C * C), F32),
        ),
        in_specs=[vmem] * 5,
        out_specs=(any_space, any_space),
        scratch_shapes=[
            pltpu.VMEM((HALF, PLANE), BF16),
            pltpu.SemaphoreType.DMA((STORES + C * C // HALF,)),
            pltpu.SemaphoreType.DMA((4, 2)),
        ],
        compiler_params=pltpu.CompilerParams(vmem_limit_bytes=6 * 2**20),
    )(*(pltpu.with_memory_space_constraint(result, pltpu.VMEM) for result in results))
    return grad_fields.reshape(1, XD, C, PLANE), grad_weight


def solution(mesh):
    placed = (
        P("dp", "pencil", None, None),
        P("dp", "pencil", None, None),
        P(None, None, "pencil", None),
    )
    return jax.shard_map(
        per_device,
        mesh=mesh,
        in_specs=placed,
        out_specs=(P("dp", "pencil", None, None), P("dp", None, "pencil", None)),
        check_vma=False,
    )
```

```python
import functools
import math

import jax
import jax.numpy as jnp
import numpy as np
from jax import lax
from jax.experimental import pallas as pl
from jax.experimental.pallas import tpu as pltpu
from jax.sharding import PartitionSpec as P

C = 32
MX = 32
MY = 32
MZ = 16
NX = 256
NY = 128
NZ = 32
PLANE = NY * NZ
PENCIL = 32
GROUPS = 8
XD = NX // PENCIL
ROWS = XD * C
SPEC = PENCIL * 2 * MZ
HALF = 128
FOLD = PLANE // 2
DEEP = MZ // 2
STORES = 8
STACKS = 8
CORES = PENCIL // STACKS
MESH = pl.DeviceIdType.MESH
F32 = jnp.float32
BF16 = jnp.bfloat16

ROOT_HALF = 0.7071067811865476
DENSITY = 0.3989422804014327


def gelu_slope(v):
    return 0.5 * (1.0 + lax.erf(v * ROOT_HALF)) + v * jnp.exp(-0.5 * v * v) * DENSITY


@functools.lru_cache(None)
def tables():
    b = np.arange(MY)[None, :, None, None]
    c = 2 * np.arange(DEEP)[None, None, :, None] + np.arange(2)[:, None, None, None]
    p = np.arange(FOLD)[None, None, None, :]
    y, z = p % NY, p // NY
    turns = ((b - MY // 2) * y * NZ + c * z * NY) % PLANE
    angle = turns * (2.0 * math.pi / PLANE)
    plane = np.stack([np.cos(angle), -np.sin(angle)], axis=2).reshape(2, SPEC // 2, FOLD)
    kx = np.arange(MX)[:, None] - MX // 2
    j = np.arange(ROWS)[None, :] // C
    phase = ((kx * j) % NX) * (2.0 * math.pi / NX)
    twiddle = np.stack([np.cos(phase), np.sin(phase)], axis=1)
    lane = np.arange(HALF)
    pairs = np.arange(C * C)
    wide = (lane[:, None] % C) == (pairs[None, :] // C)
    again = (lane[:, None] % C) == (lane[None, :] % C)
    spread = np.tile(np.concatenate([wide, again], axis=1), (2, 1))
    first = wide * (lane[:, None] < C)
    gather = (pairs[:, None] // C) == (lane[None, :] % C)
    order = np.arange(HALF).reshape(4, 2, DEEP, 2).transpose(3, 0, 1, 2).reshape(-1)
    parity = np.zeros((HALF, HALF))
    parity[np.arange(HALF), order] = 1.0
    return (
        plane.astype(jnp.bfloat16),
        twiddle.astype(np.float32),
        spread.astype(jnp.bfloat16),
        first.astype(jnp.bfloat16),
        gather.astype(jnp.bfloat16),
        parity.astype(jnp.bfloat16),
    )


def times(value, angle, sign):
    re, im = value
    if angle == 0:
        return value
    co, si = math.cos(2 * math.pi * angle), sign * math.sin(2 * math.pi * angle)
    if angle in (0.125, 0.375):
        root = math.sqrt(0.5)
        if angle == 0.125:
            if sign > 0:
                return (re - im) * root, (re + im) * root
            return (re + im) * root, (im - re) * root
        if sign > 0:
            return (re + im) * (-root), (re - im) * root
        return (im - re) * root, (re + im) * (-root)
    return re * co - im * si, re * si + im * co


def add(a, b):
    return a[0] + b[0], a[1] + b[1]


def sub(a, b):
    return a[0] - b[0], a[1] - b[1]


def fft(values, sign):
    n = len(values)
    if n == 1:
        return values
    even, odd = fft(values[0::2], sign), fft(values[1::2], sign)
    out = [None] * n
    for k in range(n // 2):
        if k * 4 == n:
            re, im = odd[k]
            turned = (-im, re) if sign > 0 else (im, -re)
        else:
            turned = times(odd[k], k / n, sign)
        out[k] = add(even[k], turned)
        out[k + n // 2] = sub(even[k], turned)
    return out


def dot(a, b, dims):
    return lax.dot_general(a, b, (dims, ((), ())), preferred_element_type=F32)


def halves(value):
    high = value.astype(BF16)
    low = (value - high.astype(F32)).astype(BF16)
    return jnp.concatenate([high, low], axis=1)


def kernel(
    x_hbm, cot_hbm, w_hbm, table_hbm, tw_hbm, spread_hbm, first_hbm, gather_hbm, parity_hbm,
    out_ref, gw_ref, odd_table, even, tail_ref,
    x_ref, cot_ref, w_ref, even_table, tw_ref, spread_ref, first_ref, gather_ref, parity_ref,
    send, recv, folded, weight, acc, spec, terms, mixed, dx, dg,
    x_sem, table_sem, load_sem, own_sem, send_sem, recv_sem, dp_send, dp_recv, dp_own, ready_sem,
):
    table = (even_table, odd_table)
    me = lax.axis_index("pencil")
    group = lax.axis_index("dp")
    stack, core = me // CORES, lax.rem(me, CORES)

    width = 512
    blocks = FOLD // width
    lines_stack = CORES * 2 * DEEP

    def stack_at(step):
        offset = STACKS // 2 + ((step + 1) // 2) * (2 * lax.rem(step, 2) - 1)
        return lax.rem(stack + offset + STACKS, STACKS)

    def stack_lines(step):
        return pl.ds(pl.multiple_of(stack_at(jnp.int32(step)) * lines_stack, lines_stack), lines_stack)

    load_x = []
    for step in range(blocks):
        for far in range(2):
            lanes = pl.ds(far * FOLD + step * width, width)
            load_x.append(
                pltpu.make_async_copy(x_hbm.at[:, lanes], x_ref.at[:, lanes], x_sem.at[step, far])
            )
    load_table = [
        pltpu.make_async_copy(
            table_hbm.at[0, stack_lines(step)], even_table.at[stack_lines(step)], table_sem.at[step]
        )
        for step in range(STACKS)
    ]
    loads = [
        pltpu.make_async_copy(source, target, load_sem.at[place])
        for place, (source, target) in enumerate(
            [
                (table_hbm.at[1], odd_table),
                (parity_hbm, parity_ref),
                (w_hbm, w_ref),
                (tw_hbm, tw_ref),
                (spread_hbm, spread_ref),
                (gather_hbm, gather_ref),
                (first_hbm, first_ref),
                (cot_hbm, cot_ref),
            ]
        )
    ]
    for load in load_x + load_table:
        load.start()

    barrier = pltpu.get_barrier_semaphore()

    def greet_pencil(i, carry):
        pl.semaphore_signal(
            barrier, inc=1, device_id=(group, lax.rem(me + i, PENCIL)), device_id_type=MESH
        )
        return carry

    def greet_group(peer, carry):
        pl.semaphore_signal(barrier, inc=1, device_id=(peer, me), device_id_type=MESH)
        return carry

    def answer_group(peer, carry):
        pl.semaphore_signal(ready_sem, inc=1, device_id=(peer, me), device_id_type=MESH)
        return carry

    lax.fori_loop(1, PENCIL, greet_pencil, 0)
    lax.fori_loop(group + 1, GROUPS, greet_group, 0)

    def block(ref, phase, parity, part, places):
        if part is None:
            return ref.at[phase, parity, places]
        return ref.at[phase, parity, places, part]

    def post(phase, parity, part, peer):
        slot = part or 0
        pltpu.make_async_remote_copy(
            src_ref=block(send, phase, parity, part, peer),
            dst_ref=block(recv, phase, parity, part, me),
            send_sem=send_sem.at[phase, parity, slot],
            recv_sem=recv_sem.at[phase, parity, slot],
            device_id=(group, peer),
            device_id_type=MESH,
        ).start()

    def own_copy(phase, parity, part):
        return pltpu.make_async_copy(
            block(send, phase, parity, part, me),
            block(recv, phase, parity, part, me),
            own_sem.at[phase, parity, part or 0],
        )

    def arrived(phase, parity, part):
        whole = block(recv, phase, parity, part, pl.ds(0, PENCIL - 1))
        pltpu.make_async_copy(whole, whole, recv_sem.at[phase, parity, part or 0]).wait()
        own_copy(phase, parity, part).wait()

    def sent(phase, parity, part):
        whole = block(send, phase, parity, part, pl.ds(0, PENCIL - 1))
        pltpu.make_async_copy(whole, whole, send_sem.at[phase, parity, part or 0]).wait()

    def post_stacks(phase, parity, part, steps):
        def one(i, carry):
            peer = stack_at(i // CORES) * CORES + lax.rem(core + i, CORES)

            @pl.when(peer != me)
            def _():
                post(phase, parity, part, peer)

            return carry

        lax.fori_loop(steps[0] * CORES, steps[1] * CORES, one, 0)

    def post_all(phase, parity, part):
        post_stacks(phase, parity, part, (0, STACKS))
        own_copy(phase, parity, part).start()

    def plane_forward(source, phase, parity, part, ready=None, before_post=None):
        pieces = 2
        each = STACKS // pieces
        for piece in range(pieces):
            steps = range(piece * each, (piece + 1) * each)
            if ready is not None:
                for step in steps:
                    ready[step].wait()
            lines = jnp.concatenate([table[parity][stack_lines(step)] for step in steps], axis=0)
            result = dot(lines, source, ((1,), (1,))).astype(BF16)
            for k, step in enumerate(steps):
                mine = result[k * lines_stack : (k + 1) * lines_stack]
                places = pl.ds(stack_at(jnp.int32(step)) * CORES, CORES)
                for place, half in enumerate((0, 1) if part is None else (part,)):
                    send[phase, parity, places, half] = mine[
                        :, place * HALF : (place + 1) * HALF
                    ].reshape(CORES, 2 * DEEP, HALF)
            if before_post is not None and piece == 0:
                before_post()
            post_stacks(phase, parity, part, (piece * each, (piece + 1) * each))
        own_copy(phase, parity, part).start()

    def first_forward(phase, parity, half):
        values = []
        for d in range(PENCIL):
            both = recv[phase, parity, d, half].astype(F32)
            values.append((both[:DEEP], both[DEEP:]))
        spectrum = fft(values, -1)
        for a in range(MX):
            re, im = spectrum[(a - MX // 2) % MX]
            co = tw_ref[a, 0:1, half * HALF : (half + 1) * HALF]
            si = tw_ref[a, 1:2, half * HALF : (half + 1) * HALF]
            for r, value in enumerate((re * co + im * si, im * co - re * si)):
                rows = slice(r * DEEP, (r + 1) * DEEP)
                acc[parity, a, rows] = value if half == 0 else acc[parity, a, rows] + value

    def first_inverse(phase, parity, half, scale):
        values = [None] * MX
        for a in range(MX):
            re, im = mixed[a, :DEEP], mixed[a, DEEP:]
            co = tw_ref[a, 0:1, half * HALF : (half + 1) * HALF]
            si = tw_ref[a, 1:2, half * HALF : (half + 1) * HALF]
            values[(a - MX // 2) % MX] = (re * co - im * si, im * co + re * si)
        signal = fft(values, 1)
        for d in range(PENCIL):
            both = jnp.concatenate(signal[d], axis=0)
            if scale is not None:
                both = both * scale
            send[phase, parity, d, half] = both.astype(BF16)

    mine_a = MX // GROUPS

    def share_own(source, target, which, parity):
        return pltpu.make_async_copy(
            source.at[parity, pl.ds(group * mine_a, mine_a)],
            target.at[parity, group],
            dp_own.at[which, parity],
        )

    def share(source, target, which, parity):
        def one(i, carry):
            peer = lax.rem(group + i, GROUPS)
            pltpu.make_async_remote_copy(
                src_ref=source.at[parity, pl.ds(peer * mine_a, mine_a)],
                dst_ref=target.at[parity, group],
                send_sem=dp_send.at[which, parity],
                recv_sem=dp_recv.at[which, parity],
                device_id=(peer, me),
                device_id_type=MESH,
            ).start()
            return carry

        lax.fori_loop(1, GROUPS, one, 0)
        share_own(source, target, which, parity).start()

    def shared(source, target, which, parity):
        whole = target.at[parity, pl.ds(0, GROUPS - 1)]
        pltpu.make_async_copy(whole, whole, dp_recv.at[which, parity]).wait()
        pltpu.make_async_copy(whole, whole, dp_send.at[which, parity]).wait()
        share_own(source, target, which, parity).wait()

    depth = lax.rem(lax.broadcasted_iota(jnp.int32, (2 * DEEP, HALF), 0), DEEP)
    volume = 1.0 / (NX * NY * NZ)
    scales = (
        jnp.where(depth == 0, volume, 2.0 * volume).astype(F32),
        jnp.full((2 * DEEP, HALF), 2.0 * volume, F32),
    )
    block_a = 8
    block_rows = block_a * 2 * DEEP
    lane_tiles = [slice(t * HALF, (t + 1) * HALF) for t in range(C * C // HALF)]

    def forward_mix(parity):
        def one(step, carry):
            own_a = pl.ds(step * block_a, block_a)
            lines = halves(acc[parity, own_a].reshape(block_rows, HALF))
            wide = dot(lines, spread_ref[...], ((1,), (0,)))
            spec[parity, own_a] = (
                wide[:, C * C :].astype(BF16).reshape(block_a, 2 * DEEP, HALF)
            )
            totals = []
            for a in range(block_a):
                out_re = jnp.zeros((DEEP, HALF), F32)
                out_im = jnp.zeros((DEEP, HALF), F32)
                row = a * 2 * DEEP
                for lanes in lane_tiles:
                    w_re = weight[parity, step * block_a + a, :DEEP, lanes]
                    w_im = weight[parity, step * block_a + a, DEEP:, lanes]
                    x_re = wide[row : row + DEEP, lanes]
                    x_im = wide[row + DEEP : row + 2 * DEEP, lanes]
                    out_re = out_re + x_re * w_re - x_im * w_im
                    out_im = out_im + x_re * w_im + x_im * w_re
                totals += [out_re, out_im]
            sums = dot(halves(jnp.concatenate(totals, axis=0)), spread_ref[:, C * C :], ((1,), (0,)))
            mixed[own_a] = sums.reshape(block_a, 2 * DEEP, HALF)
            return carry

        lax.fori_loop(0, MX // block_a, one, 0, unroll=2)

    def backward_mix(parity):
        def one(step, carry):
            own_a = pl.ds(step * block_a, block_a)
            lines = halves(acc[parity, own_a].reshape(block_rows, HALF))
            sums = dot(lines, spread_ref[:, C * C :], ((1,), (0,)))
            narrow = (sums.reshape(block_a, 2 * DEEP, HALF) * scales[parity]).astype(BF16)
            terms[parity, own_a] = narrow
            grads = narrow.astype(F32)
            products = []
            for a in range(block_a):
                g_re, g_im = grads[a, :DEEP], grads[a, DEEP:]
                tiles = []
                for lanes in lane_tiles:
                    w_re = weight[parity, step * block_a + a, :DEEP, lanes]
                    w_im = weight[parity, step * block_a + a, DEEP:, lanes]
                    tiles.append(
                        jnp.concatenate(
                            [g_re * w_re + g_im * w_im, g_im * w_re - g_re * w_im], axis=0
                        ).astype(BF16)
                    )
                products.append(jnp.concatenate(tiles, axis=1))
            result = dot(jnp.concatenate(products, axis=0), gather_ref[...], ((1,), (0,)))
            mixed[own_a] = result.reshape(block_a, 2 * DEEP, HALF)
            return carry

        lax.fori_loop(0, MX // block_a, one, 0, unroll=2)

    def lines_of(phase, parity, half):
        return recv[phase, parity, :, half].reshape(SPEC // 2, HALF)

    def even_cells(phase, half):
        if half is None:
            lines = jnp.concatenate([lines_of(phase, 0, 0), lines_of(phase, 0, 1)], axis=1).T
            rows = pl.ds(0, ROWS)
        else:
            lines = lines_of(phase, 0, half).T
            rows = pl.ds(half * HALF, HALF)

        def one(step, carry):
            lanes = pl.ds(pl.multiple_of(step * width, width), width)
            even[rows, lanes] = dot(lines, even_table[:, lanes], ((1,), (0,)))
            return carry

        lax.fori_loop(0, FOLD // width, one, 0)

    def odd_cells(phase, half, finish):
        lines = lines_of(phase, 1, half).T
        rows = pl.ds(half * HALF, HALF)

        def one(step, carry):
            near = pl.ds(pl.multiple_of(step * width, width), width)
            far = pl.ds(pl.multiple_of(FOLD + step * width, width), width)
            odd = dot(lines, odd_table[:, near], ((1,), (0,)))
            base = even[rows, near]
            finish(rows, near, far, base + odd, base - odd)
            return carry

        lax.fori_loop(0, FOLD // width, one, 0, unroll=True)

    for step in range(blocks):
        near, far = pl.ds(step * width, width), pl.ds(FOLD + step * width, width)
        load_x[2 * step].wait()
        load_x[2 * step + 1].wait()
        one, two = x_ref[:, near], x_ref[:, far]
        folded[0, :, near] = one + two
        folded[1, :, near] = one - two
    for load in loads:
        load.start()

    def all_here():
        pl.semaphore_wait(barrier, PENCIL - 1 + group)

    plane_forward(folded[0], 0, 0, None, load_table, all_here)
    loads[0].wait()
    plane_forward(folded[1], 0, 1, None)
    lax.fori_loop(0, group, answer_group, 0)

    loads[1].wait()
    loads[2].wait()

    def part_weights(step, carry):
        own_a = pl.ds(step * 4, 4)
        lines = w_ref[own_a].reshape(HALF, C * C)
        apart = dot(parity_ref[...], lines, ((1,), (0,)))
        for parity in range(2):
            weight[parity, own_a] = apart[parity * HALF // 2 : (parity + 1) * HALF // 2].reshape(
                4, 2 * DEEP, C * C
            )
        return carry

    lax.fori_loop(0, MX // 4, part_weights, 0)
    for load in loads[3:]:
        load.wait()

    for parity in range(2):
        arrived(0, parity, None)
        for half in range(2):
            first_forward(0, parity, half)
        forward_mix(parity)
        for half in range(2):
            first_inverse(1, parity, half, scales[parity])
            if half == 0:
                post_all(1, parity, 0)
    for parity in range(2):
        post_all(1, parity, 1)


    def slopes(rows, near, far, one, two):
        one = gelu_slope(one) * cot_ref[rows, near].astype(F32)
        two = gelu_slope(two) * cot_ref[rows, far].astype(F32)
        folded[0, rows, near] = (one + two).astype(BF16)
        folded[1, rows, near] = (one - two).astype(BF16)

    for half in range(2):
        arrived(1, 0, half)
        even_cells(1, half)
        arrived(1, 1, half)
        odd_cells(1, half, slopes)
        for parity in range(2):
            plane_forward(folded[parity, pl.ds(half * HALF, HALF)], 2, parity, half)

    @pl.when(group < GROUPS - 1)
    def _():
        pl.semaphore_wait(ready_sem, GROUPS - 1 - group)

    for parity in range(2):
        share(spec, dx, 0, parity)

    for parity in range(2):
        arrived(2, parity, 0)
        first_forward(2, parity, 0)
    for parity in range(2):
        arrived(2, parity, 1)
        first_forward(2, parity, 1)
        backward_mix(parity)
        share(terms, dg, 1, parity)
        for half in range(2):
            first_inverse(3, parity, half, None)
            if parity == 1:
                post_all(3, parity, half)
        if parity == 0:
            post_all(3, parity, None)

    arrived(3, 0, None)
    even_cells(3, None)

    for parity in range(2):
        shared(spec, dx, 0, parity)
        shared(terms, dg, 1, parity)

    def outer(a, carry):
        for parity in range(2):
            lines = dx[parity, :, a].reshape(HALF, HALF)
            wide = dot(lines, first_ref[...], ((1,), (0,)))
            factors = [dg[parity, s, a].astype(F32) for s in range(GROUPS)]
            for tile, lanes in enumerate(lane_tiles):
                out_re = jnp.zeros((DEEP, HALF), F32)
                out_im = jnp.zeros((DEEP, HALF), F32)
                for s in range(GROUPS):
                    row = s * 2 * DEEP
                    x_re, x_im = wide[row : row + DEEP, lanes], wide[row + DEEP : row + 2 * DEEP, lanes]
                    g_re, g_im = factors[s][:DEEP], factors[s][DEEP:]
                    out_re = out_re + x_re * g_re + x_im * g_im
                    out_im = out_im + x_re * g_im - x_im * g_re
                gw_ref[tile, a, 0, pl.ds(parity, DEEP, stride=2)] = out_re
                gw_ref[tile, a, 1, pl.ds(parity, DEEP, stride=2)] = out_im
        return carry

    lax.fori_loop(0, MX // GROUPS, outer, 0, unroll=2)


    def finish(rows, near, far, one, two):
        out_ref[rows, near] = one.astype(BF16)
        out_ref[rows, far] = two.astype(BF16)

    arrived(3, 1, 0)
    odd_cells(3, 0, finish)
    arrived(3, 1, 1)
    tail_ref[...] = lines_of(3, 1, 1).T

    for parity in range(2):
        sent(0, parity, None)
        for half in range(2):
            sent(2, parity, half)
        for half in range(2):
            sent(1, parity, half)
    sent(3, 0, None)
    for half in range(2):
        sent(3, 1, half)


def last_kernel(
    out_ref, gw_ref, table_ref, even_ref, lines_ref, out_hbm, gw_hbm, tail, store_sem, tail_sem
):
    stores = []
    for place in range(STORES):
        rows = pl.ds(place * (HALF // STORES), HALF // STORES)
        stores.append(
            pltpu.make_async_copy(out_ref.at[rows], out_hbm.at[rows], store_sem.at[place])
        )
    for tile in range(C * C // HALF):
        lanes = slice(tile * HALF, (tile + 1) * HALF)
        stores.append(
            pltpu.make_async_copy(
                gw_ref.at[tile], gw_hbm.at[:, :, :, lanes], store_sem.at[STORES + tile]
            )
        )
    for store in stores:
        store.start()
    width = 512
    rows = pl.ds(HALF, HALF)
    for step in range(FOLD // width):
        near, far = pl.ds(step * width, width), pl.ds(FOLD + step * width, width)
        odd = dot(lines_ref[...], table_ref[:, near], ((1,), (0,)))
        base = even_ref[rows, near]
        tail[:, near] = (base + odd).astype(BF16)
        tail[:, far] = (base - odd).astype(BF16)
        for place, lanes in enumerate((near, far)):
            store = pltpu.make_async_copy(
                tail.at[:, lanes], out_hbm.at[rows, lanes], tail_sem.at[step, place]
            )
            store.start()
            stores.append(store)
    for store in stores:
        store.wait()


def per_device(fields, cotangent, spectral_weight):
    any_space = pl.BlockSpec(memory_space=pl.ANY)
    vmem = pl.BlockSpec(memory_space=pltpu.VMEM)
    messages = (4, 2, PENCIL, 2, 2 * DEEP, HALF)
    spectrum = (2, MX, 2 * DEEP, HALF)
    mine = MX // GROUPS
    constants = [jnp.asarray(table) for table in tables()]
    results = pl.pallas_call(
        kernel,
        out_shape=(
            pltpu.VMEM((HALF, PLANE), BF16),
            pltpu.VMEM((C * C // HALF, mine, 2, MZ, HALF), F32),
            pltpu.VMEM((SPEC // 2, FOLD), BF16),
            pltpu.VMEM((ROWS, FOLD), F32),
            pltpu.VMEM((HALF, SPEC // 2), BF16),
        ),
        in_specs=[any_space] * (3 + len(constants)),
        out_specs=(vmem,) * 5,
        scratch_shapes=[
            pltpu.VMEM((ROWS, PLANE), BF16),
            pltpu.VMEM((ROWS, PLANE), BF16),
            pltpu.VMEM((MX, 2, MZ, C * C), BF16),
        ]
        + [pltpu.VMEM(constants[0].shape[1:], BF16)]
        + [pltpu.VMEM(table.shape, table.dtype) for table in constants[1:]]
        + [
            pltpu.VMEM(messages, BF16),
            pltpu.VMEM(messages, BF16),
            pltpu.VMEM((2, ROWS, FOLD), BF16),
            pltpu.VMEM((2, MX, 2 * DEEP, C * C), F32),
            pltpu.VMEM((2, MX, 2 * DEEP, HALF), F32),
            pltpu.VMEM(spectrum, BF16),
            pltpu.VMEM(spectrum, BF16),
            pltpu.VMEM((MX, 2 * DEEP, HALF), F32),
            pltpu.VMEM((2, GROUPS, mine, 2 * DEEP, HALF), BF16),
            pltpu.VMEM((2, GROUPS, mine, 2 * DEEP, HALF), BF16),
            pltpu.SemaphoreType.DMA((4, 2)),
            pltpu.SemaphoreType.DMA((STACKS,)),
            pltpu.SemaphoreType.DMA((8,)),
            pltpu.SemaphoreType.DMA((4, 2, 2)),
            pltpu.SemaphoreType.DMA((4, 2, 2)),
            pltpu.SemaphoreType.DMA((4, 2, 2)),
            pltpu.SemaphoreType.DMA((2, 2)),
            pltpu.SemaphoreType.DMA((2, 2)),
            pltpu.SemaphoreType.DMA((2, 2)),
            pltpu.SemaphoreType.REGULAR,
        ],
        compiler_params=pltpu.CompilerParams(
            collective_id=0, has_side_effects=True, vmem_limit_bytes=48 * 2**20
        ),
        cost_estimate=pl.CostEstimate(
            flops=5 * 10**9, bytes_accessed=16 * 2**20, transcendentals=2**21
        ),
    )(
        *(
            pltpu.with_memory_space_constraint(operand, pltpu.HBM)
            for operand in (
                fields.reshape(ROWS, PLANE),
                cotangent.reshape(ROWS, PLANE),
                spectral_weight,
                *constants,
            )
        )
    )
    grad_fields, grad_weight = pl.pallas_call(
        last_kernel,
        out_shape=(
            jax.ShapeDtypeStruct((ROWS, PLANE), BF16),
            jax.ShapeDtypeStruct((mine, 2, MZ, C * C), F32),
        ),
        in_specs=[vmem] * 5,
        out_specs=(any_space, any_space),
        scratch_shapes=[
            pltpu.VMEM((HALF, PLANE), BF16),
            pltpu.SemaphoreType.DMA((STORES + C * C // HALF,)),
            pltpu.SemaphoreType.DMA((4, 2)),
        ],
        compiler_params=pltpu.CompilerParams(vmem_limit_bytes=6 * 2**20),
    )(*(pltpu.with_memory_space_constraint(result, pltpu.VMEM) for result in results))
    return grad_fields.reshape(1, XD, C, PLANE), grad_weight


def solution(mesh):
    placed = (
        P("dp", "pencil", None, None),
        P("dp", "pencil", None, None),
        P(None, None, "pencil", None),
    )
    return jax.shard_map(
        per_device,
        mesh=mesh,
        in_specs=placed,
        out_specs=(P("dp", "pencil", None, None), P("dp", None, "pencil", None)),
        check_vma=False,
    )
```

```python
import functools
import math

import jax
import jax.numpy as jnp
import numpy as np
from jax import lax
from jax.experimental import pallas as pl
from jax.experimental.pallas import tpu as pltpu
from jax.sharding import PartitionSpec as P

C = 32
MX = 32
MY = 32
MZ = 16
NX = 256
NY = 128
NZ = 32
PLANE = NY * NZ
PENCIL = 32
GROUPS = 8
XD = NX // PENCIL
ROWS = XD * C
SPEC = PENCIL * 2 * MZ
HALF = 128
FOLD = PLANE // 2
DEEP = MZ // 2
STORES = 8
STACKS = 8
CORES = PENCIL // STACKS
MESH = pl.DeviceIdType.MESH
F32 = jnp.float32
BF16 = jnp.bfloat16

ROOT_HALF = 0.7071067811865476
DENSITY = 0.3989422804014327


def gelu_slope(v):
    return 0.5 * (1.0 + lax.erf(v * ROOT_HALF)) + v * jnp.exp(-0.5 * v * v) * DENSITY


@functools.lru_cache(None)
def tables():
    b = np.arange(MY)[None, :, None, None]
    c = 2 * np.arange(DEEP)[None, None, :, None] + np.arange(2)[:, None, None, None]
    p = np.arange(FOLD)[None, None, None, :]
    y, z = p % NY, p // NY
    turns = ((b - MY // 2) * y * NZ + c * z * NY) % PLANE
    angle = turns * (2.0 * math.pi / PLANE)
    plane = np.stack([np.cos(angle), -np.sin(angle)], axis=2).reshape(2, SPEC // 2, FOLD)
    kx = np.arange(MX)[:, None] - MX // 2
    j = np.arange(ROWS)[None, :] // C
    phase = ((kx * j) % NX) * (2.0 * math.pi / NX)
    twiddle = np.stack([np.cos(phase), np.sin(phase)], axis=1)
    lane = np.arange(HALF)
    pairs = np.arange(C * C)
    wide = (lane[:, None] % C) == (pairs[None, :] // C)
    again = (lane[:, None] % C) == (lane[None, :] % C)
    spread = np.tile(np.concatenate([wide, again], axis=1), (2, 1))
    first = wide * (lane[:, None] < C)
    gather = (pairs[:, None] // C) == (lane[None, :] % C)
    order = np.arange(HALF).reshape(4, 2, DEEP, 2).transpose(3, 0, 1, 2).reshape(-1)
    parity = np.zeros((HALF, HALF))
    parity[np.arange(HALF), order] = 1.0
    return (
        plane.astype(jnp.bfloat16),
        twiddle.astype(np.float32),
        spread.astype(jnp.bfloat16),
        first.astype(jnp.bfloat16),
        gather.astype(jnp.bfloat16),
        parity.astype(jnp.bfloat16),
    )


def times(value, angle, sign):
    re, im = value
    if angle == 0:
        return value
    co, si = math.cos(2 * math.pi * angle), sign * math.sin(2 * math.pi * angle)
    if angle in (0.125, 0.375):
        root = math.sqrt(0.5)
        if angle == 0.125:
            if sign > 0:
                return (re - im) * root, (re + im) * root
            return (re + im) * root, (im - re) * root
        if sign > 0:
            return (re + im) * (-root), (re - im) * root
        return (im - re) * root, (re + im) * (-root)
    return re * co - im * si, re * si + im * co


def add(a, b):
    return a[0] + b[0], a[1] + b[1]


def sub(a, b):
    return a[0] - b[0], a[1] - b[1]


def fft(values, sign):
    n = len(values)
    if n == 1:
        return values
    even, odd = fft(values[0::2], sign), fft(values[1::2], sign)
    out = [None] * n
    for k in range(n // 2):
        if k * 4 == n:
            re, im = odd[k]
            turned = (-im, re) if sign > 0 else (im, -re)
        else:
            turned = times(odd[k], k / n, sign)
        out[k] = add(even[k], turned)
        out[k + n // 2] = sub(even[k], turned)
    return out


def dot(a, b, dims):
    return lax.dot_general(a, b, (dims, ((), ())), preferred_element_type=F32)


def halves(value):
    high = value.astype(BF16)
    low = (value - high.astype(F32)).astype(BF16)
    return jnp.concatenate([high, low], axis=1)


def kernel(
    x_hbm, cot_hbm, w_hbm, table_hbm, tw_hbm, spread_hbm, first_hbm, gather_hbm, parity_hbm,
    out_ref, gw_ref, odd_table, even, tail_ref,
    x_ref, cot_ref, w_ref, even_table, tw_ref, spread_ref, first_ref, gather_ref, parity_ref,
    send, recv, folded, weight, acc, spec, terms, mixed, dx, dg,
    x_sem, table_sem, load_sem, own_sem, send_sem, recv_sem, dp_send, dp_recv, dp_own, ready_sem,
):
    table = (even_table, odd_table)
    me = lax.axis_index("pencil")
    group = lax.axis_index("dp")
    stack, core = me // CORES, lax.rem(me, CORES)

    width = 512
    blocks = FOLD // width
    lines_stack = CORES * 2 * DEEP

    def stack_at(step):
        offset = STACKS // 2 + ((step + 1) // 2) * (2 * lax.rem(step, 2) - 1)
        return lax.rem(stack + offset + STACKS, STACKS)

    def stack_lines(step):
        return pl.ds(pl.multiple_of(stack_at(jnp.int32(step)) * lines_stack, lines_stack), lines_stack)

    load_x = []
    for step in range(blocks):
        for far in range(2):
            lanes = pl.ds(far * FOLD + step * width, width)
            load_x.append(
                pltpu.make_async_copy(x_hbm.at[:, lanes], x_ref.at[:, lanes], x_sem.at[step, far])
            )
    load_table = [
        pltpu.make_async_copy(
            table_hbm.at[0, stack_lines(step)], even_table.at[stack_lines(step)], table_sem.at[step]
        )
        for step in range(STACKS)
    ]
    loads = [
        pltpu.make_async_copy(source, target, load_sem.at[place])
        for place, (source, target) in enumerate(
            [
                (table_hbm.at[1], odd_table),
                (parity_hbm, parity_ref),
                (w_hbm, w_ref),
                (tw_hbm, tw_ref),
                (spread_hbm, spread_ref),
                (gather_hbm, gather_ref),
                (first_hbm, first_ref),
                (cot_hbm, cot_ref),
            ]
        )
    ]
    for load in load_x + load_table:
        load.start()

    barrier = pltpu.get_barrier_semaphore()

    def greet_pencil(i, carry):
        pl.semaphore_signal(
            barrier, inc=1, device_id=(group, lax.rem(me + i, PENCIL)), device_id_type=MESH
        )
        return carry

    def greet_group(peer, carry):
        pl.semaphore_signal(barrier, inc=1, device_id=(peer, me), device_id_type=MESH)
        return carry

    def answer_group(peer, carry):
        pl.semaphore_signal(ready_sem, inc=1, device_id=(peer, me), device_id_type=MESH)
        return carry

    lax.fori_loop(1, PENCIL, greet_pencil, 0)
    lax.fori_loop(group + 1, GROUPS, greet_group, 0)

    def block(ref, phase, parity, part, places):
        if part is None:
            return ref.at[phase, parity, places]
        return ref.at[phase, parity, places, part]

    def post(phase, parity, part, peer):
        slot = part or 0
        pltpu.make_async_remote_copy(
            src_ref=block(send, phase, parity, part, peer),
            dst_ref=block(recv, phase, parity, part, me),
            send_sem=send_sem.at[phase, parity, slot],
            recv_sem=recv_sem.at[phase, parity, slot],
            device_id=(group, peer),
            device_id_type=MESH,
        ).start()

    def own_copy(phase, parity, part):
        return pltpu.make_async_copy(
            block(send, phase, parity, part, me),
            block(recv, phase, parity, part, me),
            own_sem.at[phase, parity, part or 0],
        )

    def arrived(phase, parity, part):
        whole = block(recv, phase, parity, part, pl.ds(0, PENCIL - 1))
        pltpu.make_async_copy(whole, whole, recv_sem.at[phase, parity, part or 0]).wait()
        own_copy(phase, parity, part).wait()

    def sent(phase, parity, part):
        whole = block(send, phase, parity, part, pl.ds(0, PENCIL - 1))
        pltpu.make_async_copy(whole, whole, send_sem.at[phase, parity, part or 0]).wait()

    ring = [lax.rem(core + k, CORES) for k in range(CORES)]

    def post_stacks(phase, parity, part, steps):
        def one(step, carry):
            base = stack_at(step) * CORES
            for place in ring:
                post(phase, parity, part, base + place)
            return carry

        lax.fori_loop(steps[0], min(steps[1], STACKS - 1), one, 0)
        if steps[1] == STACKS:
            for place in ring[1:]:
                post(phase, parity, part, stack * CORES + place)

    def post_all(phase, parity, part):
        post_stacks(phase, parity, part, (0, STACKS))
        own_copy(phase, parity, part).start()

    def plane_forward(source, phase, parity, part, ready=None, before_post=None):
        pieces = 2
        each = STACKS // pieces
        for piece in range(pieces):
            steps = range(piece * each, (piece + 1) * each)
            if ready is not None:
                for step in steps:
                    ready[step].wait()
            lines = jnp.concatenate([table[parity][stack_lines(step)] for step in steps], axis=0)
            result = dot(lines, source, ((1,), (1,))).astype(BF16)
            for k, step in enumerate(steps):
                mine = result[k * lines_stack : (k + 1) * lines_stack]
                places = pl.ds(stack_at(jnp.int32(step)) * CORES, CORES)
                for place, half in enumerate((0, 1) if part is None else (part,)):
                    send[phase, parity, places, half] = mine[
                        :, place * HALF : (place + 1) * HALF
                    ].reshape(CORES, 2 * DEEP, HALF)
            if before_post is not None and piece == 0:
                before_post()
            post_stacks(phase, parity, part, (piece * each, (piece + 1) * each))
        own_copy(phase, parity, part).start()

    def first_forward(phase, parity, half):
        values = []
        for d in range(PENCIL):
            both = recv[phase, parity, d, half].astype(F32)
            values.append((both[:DEEP], both[DEEP:]))
        spectrum = fft(values, -1)
        for a in range(MX):
            re, im = spectrum[(a - MX // 2) % MX]
            co = tw_ref[a, 0:1, half * HALF : (half + 1) * HALF]
            si = tw_ref[a, 1:2, half * HALF : (half + 1) * HALF]
            for r, value in enumerate((re * co + im * si, im * co - re * si)):
                rows = slice(r * DEEP, (r + 1) * DEEP)
                acc[parity, a, rows] = value if half == 0 else acc[parity, a, rows] + value

    def first_inverse(phase, parity, half, scale):
        values = [None] * MX
        for a in range(MX):
            re, im = mixed[a, :DEEP], mixed[a, DEEP:]
            co = tw_ref[a, 0:1, half * HALF : (half + 1) * HALF]
            si = tw_ref[a, 1:2, half * HALF : (half + 1) * HALF]
            values[(a - MX // 2) % MX] = (re * co - im * si, im * co + re * si)
        signal = fft(values, 1)
        for d in range(PENCIL):
            both = jnp.concatenate(signal[d], axis=0)
            if scale is not None:
                both = both * scale
            send[phase, parity, d, half] = both.astype(BF16)

    mine_a = MX // GROUPS

    def share_own(source, target, which, parity):
        return pltpu.make_async_copy(
            source.at[parity, pl.ds(group * mine_a, mine_a)],
            target.at[parity, group],
            dp_own.at[which, parity],
        )

    def share(source, target, which, parity):
        def one(i, carry):
            peer = lax.rem(group + i, GROUPS)
            pltpu.make_async_remote_copy(
                src_ref=source.at[parity, pl.ds(peer * mine_a, mine_a)],
                dst_ref=target.at[parity, group],
                send_sem=dp_send.at[which, parity],
                recv_sem=dp_recv.at[which, parity],
                device_id=(peer, me),
                device_id_type=MESH,
            ).start()
            return carry

        lax.fori_loop(1, GROUPS, one, 0)
        share_own(source, target, which, parity).start()

    def shared(source, target, which, parity):
        whole = target.at[parity, pl.ds(0, GROUPS - 1)]
        pltpu.make_async_copy(whole, whole, dp_recv.at[which, parity]).wait()
        pltpu.make_async_copy(whole, whole, dp_send.at[which, parity]).wait()
        share_own(source, target, which, parity).wait()

    depth = lax.rem(lax.broadcasted_iota(jnp.int32, (2 * DEEP, HALF), 0), DEEP)
    volume = 1.0 / (NX * NY * NZ)
    scales = (
        jnp.where(depth == 0, volume, 2.0 * volume).astype(F32),
        jnp.full((2 * DEEP, HALF), 2.0 * volume, F32),
    )
    block_a = 8
    block_rows = block_a * 2 * DEEP
    lane_tiles = [slice(t * HALF, (t + 1) * HALF) for t in range(C * C // HALF)]

    def forward_mix(parity):
        def one(step, carry):
            own_a = pl.ds(step * block_a, block_a)
            lines = halves(acc[parity, own_a].reshape(block_rows, HALF))
            wide = dot(lines, spread_ref[...], ((1,), (0,)))
            spec[parity, own_a] = (
                wide[:, C * C :].astype(BF16).reshape(block_a, 2 * DEEP, HALF)
            )
            totals = []
            for a in range(block_a):
                out_re = jnp.zeros((DEEP, HALF), F32)
                out_im = jnp.zeros((DEEP, HALF), F32)
                row = a * 2 * DEEP
                for lanes in lane_tiles:
                    w_re = weight[parity, step * block_a + a, :DEEP, lanes]
                    w_im = weight[parity, step * block_a + a, DEEP:, lanes]
                    x_re = wide[row : row + DEEP, lanes]
                    x_im = wide[row + DEEP : row + 2 * DEEP, lanes]
                    out_re = out_re + x_re * w_re - x_im * w_im
                    out_im = out_im + x_re * w_im + x_im * w_re
                totals += [out_re, out_im]
            sums = dot(halves(jnp.concatenate(totals, axis=0)), spread_ref[:, C * C :], ((1,), (0,)))
            mixed[own_a] = sums.reshape(block_a, 2 * DEEP, HALF)
            return carry

        lax.fori_loop(0, MX // block_a, one, 0, unroll=2)

    def backward_mix(parity):
        def one(step, carry):
            own_a = pl.ds(step * block_a, block_a)
            lines = halves(acc[parity, own_a].reshape(block_rows, HALF))
            sums = dot(lines, spread_ref[:, C * C :], ((1,), (0,)))
            narrow = (sums.reshape(block_a, 2 * DEEP, HALF) * scales[parity]).astype(BF16)
            terms[parity, own_a] = narrow
            grads = narrow.astype(F32)
            products = []
            for a in range(block_a):
                g_re, g_im = grads[a, :DEEP], grads[a, DEEP:]
                tiles = []
                for lanes in lane_tiles:
                    w_re = weight[parity, step * block_a + a, :DEEP, lanes]
                    w_im = weight[parity, step * block_a + a, DEEP:, lanes]
                    tiles.append(
                        jnp.concatenate(
                            [g_re * w_re + g_im * w_im, g_im * w_re - g_re * w_im], axis=0
                        ).astype(BF16)
                    )
                products.append(jnp.concatenate(tiles, axis=1))
            result = dot(jnp.concatenate(products, axis=0), gather_ref[...], ((1,), (0,)))
            mixed[own_a] = result.reshape(block_a, 2 * DEEP, HALF)
            return carry

        lax.fori_loop(0, MX // block_a, one, 0, unroll=2)

    def lines_of(phase, parity, half):
        return recv[phase, parity, :, half].reshape(SPEC // 2, HALF)

    def even_cells(phase, half):
        if half is None:
            lines = jnp.concatenate([lines_of(phase, 0, 0), lines_of(phase, 0, 1)], axis=1).T
            rows = pl.ds(0, ROWS)
        else:
            lines = lines_of(phase, 0, half).T
            rows = pl.ds(half * HALF, HALF)

        def one(step, carry):
            lanes = pl.ds(pl.multiple_of(step * width, width), width)
            even[rows, lanes] = dot(lines, even_table[:, lanes], ((1,), (0,)))
            return carry

        lax.fori_loop(0, FOLD // width, one, 0)

    def odd_cells(phase, half, finish):
        lines = lines_of(phase, 1, half).T
        rows = pl.ds(half * HALF, HALF)

        def one(step, carry):
            near = pl.ds(pl.multiple_of(step * width, width), width)
            far = pl.ds(pl.multiple_of(FOLD + step * width, width), width)
            odd = dot(lines, odd_table[:, near], ((1,), (0,)))
            base = even[rows, near]
            finish(rows, near, far, base + odd, base - odd)
            return carry

        lax.fori_loop(0, FOLD // width, one, 0, unroll=True)

    for step in range(blocks):
        near, far = pl.ds(step * width, width), pl.ds(FOLD + step * width, width)
        load_x[2 * step].wait()
        load_x[2 * step + 1].wait()
        one, two = x_ref[:, near], x_ref[:, far]
        folded[0, :, near] = one + two
        folded[1, :, near] = one - two
    for load in loads:
        load.start()

    def all_here():
        pl.semaphore_wait(barrier, PENCIL - 1 + group)

    plane_forward(folded[0], 0, 0, None, load_table, all_here)
    loads[0].wait()
    plane_forward(folded[1], 0, 1, None)
    lax.fori_loop(0, group, answer_group, 0)

    loads[1].wait()
    loads[2].wait()

    def part_weights(step, carry):
        own_a = pl.ds(step * 4, 4)
        lines = w_ref[own_a].reshape(HALF, C * C)
        apart = dot(parity_ref[...], lines, ((1,), (0,)))
        for parity in range(2):
            weight[parity, own_a] = apart[parity * HALF // 2 : (parity + 1) * HALF // 2].reshape(
                4, 2 * DEEP, C * C
            )
        return carry

    lax.fori_loop(0, MX // 4, part_weights, 0)
    for load in loads[3:]:
        load.wait()

    for parity in range(2):
        arrived(0, parity, None)
        for half in range(2):
            first_forward(0, parity, half)
        forward_mix(parity)
        for half in range(2):
            first_inverse(1, parity, half, scales[parity])
            if half == 0:
                post_all(1, parity, 0)
    for parity in range(2):
        post_all(1, parity, 1)


    def slopes(rows, near, far, one, two):
        one = gelu_slope(one) * cot_ref[rows, near].astype(F32)
        two = gelu_slope(two) * cot_ref[rows, far].astype(F32)
        folded[0, rows, near] = (one + two).astype(BF16)
        folded[1, rows, near] = (one - two).astype(BF16)

    for half in range(2):
        arrived(1, 0, half)
        even_cells(1, half)
        arrived(1, 1, half)
        odd_cells(1, half, slopes)
        for parity in range(2):
            plane_forward(folded[parity, pl.ds(half * HALF, HALF)], 2, parity, half)

    @pl.when(group < GROUPS - 1)
    def _():
        pl.semaphore_wait(ready_sem, GROUPS - 1 - group)

    for parity in range(2):
        share(spec, dx, 0, parity)

    for parity in range(2):
        arrived(2, parity, 0)
        first_forward(2, parity, 0)
    for parity in range(2):
        arrived(2, parity, 1)
        first_forward(2, parity, 1)
        backward_mix(parity)
        share(terms, dg, 1, parity)
        for half in range(2):
            first_inverse(3, parity, half, None)
            if parity == 1:
                post_all(3, parity, half)
        if parity == 0:
            post_all(3, parity, None)

    arrived(3, 0, None)
    even_cells(3, None)

    for parity in range(2):
        shared(spec, dx, 0, parity)
        shared(terms, dg, 1, parity)

    def outer(a, carry):
        for parity in range(2):
            lines = dx[parity, :, a].reshape(HALF, HALF)
            wide = dot(lines, first_ref[...], ((1,), (0,)))
            factors = [dg[parity, s, a].astype(F32) for s in range(GROUPS)]
            for tile, lanes in enumerate(lane_tiles):
                out_re = jnp.zeros((DEEP, HALF), F32)
                out_im = jnp.zeros((DEEP, HALF), F32)
                for s in range(GROUPS):
                    row = s * 2 * DEEP
                    x_re, x_im = wide[row : row + DEEP, lanes], wide[row + DEEP : row + 2 * DEEP, lanes]
                    g_re, g_im = factors[s][:DEEP], factors[s][DEEP:]
                    out_re = out_re + x_re * g_re + x_im * g_im
                    out_im = out_im + x_re * g_im - x_im * g_re
                gw_ref[tile, a, 0, pl.ds(parity, DEEP, stride=2)] = out_re
                gw_ref[tile, a, 1, pl.ds(parity, DEEP, stride=2)] = out_im
        return carry

    lax.fori_loop(0, MX // GROUPS, outer, 0, unroll=2)


    def finish(rows, near, far, one, two):
        out_ref[rows, near] = one.astype(BF16)
        out_ref[rows, far] = two.astype(BF16)

    arrived(3, 1, 0)
    odd_cells(3, 0, finish)
    arrived(3, 1, 1)
    tail_ref[...] = lines_of(3, 1, 1).T

    for parity in range(2):
        sent(0, parity, None)
        for half in range(2):
            sent(2, parity, half)
        for half in range(2):
            sent(1, parity, half)
    sent(3, 0, None)
    for half in range(2):
        sent(3, 1, half)


def last_kernel(
    out_ref, gw_ref, table_ref, even_ref, lines_ref, out_hbm, gw_hbm, tail, store_sem, tail_sem
):
    stores = []
    for place in range(STORES):
        rows = pl.ds(place * (HALF // STORES), HALF // STORES)
        stores.append(
            pltpu.make_async_copy(out_ref.at[rows], out_hbm.at[rows], store_sem.at[place])
        )
    for tile in range(C * C // HALF):
        lanes = slice(tile * HALF, (tile + 1) * HALF)
        stores.append(
            pltpu.make_async_copy(
                gw_ref.at[tile], gw_hbm.at[:, :, :, lanes], store_sem.at[STORES + tile]
            )
        )
    for store in stores:
        store.start()
    width = 512
    rows = pl.ds(HALF, HALF)
    for step in range(FOLD // width):
        near, far = pl.ds(step * width, width), pl.ds(FOLD + step * width, width)
        odd = dot(lines_ref[...], table_ref[:, near], ((1,), (0,)))
        base = even_ref[rows, near]
        tail[:, near] = (base + odd).astype(BF16)
        tail[:, far] = (base - odd).astype(BF16)
        for place, lanes in enumerate((near, far)):
            store = pltpu.make_async_copy(
                tail.at[:, lanes], out_hbm.at[rows, lanes], tail_sem.at[step, place]
            )
            store.start()
            stores.append(store)
    for store in stores:
        store.wait()


def per_device(fields, cotangent, spectral_weight):
    any_space = pl.BlockSpec(memory_space=pl.ANY)
    vmem = pl.BlockSpec(memory_space=pltpu.VMEM)
    messages = (4, 2, PENCIL, 2, 2 * DEEP, HALF)
    spectrum = (2, MX, 2 * DEEP, HALF)
    mine = MX // GROUPS
    constants = [jnp.asarray(table) for table in tables()]
    results = pl.pallas_call(
        kernel,
        out_shape=(
            pltpu.VMEM((HALF, PLANE), BF16),
            pltpu.VMEM((C * C // HALF, mine, 2, MZ, HALF), F32),
            pltpu.VMEM((SPEC // 2, FOLD), BF16),
            pltpu.VMEM((ROWS, FOLD), F32),
            pltpu.VMEM((HALF, SPEC // 2), BF16),
        ),
        in_specs=[any_space] * (3 + len(constants)),
        out_specs=(vmem,) * 5,
        scratch_shapes=[
            pltpu.VMEM((ROWS, PLANE), BF16),
            pltpu.VMEM((ROWS, PLANE), BF16),
            pltpu.VMEM((MX, 2, MZ, C * C), BF16),
        ]
        + [pltpu.VMEM(constants[0].shape[1:], BF16)]
        + [pltpu.VMEM(table.shape, table.dtype) for table in constants[1:]]
        + [
            pltpu.VMEM(messages, BF16),
            pltpu.VMEM(messages, BF16),
            pltpu.VMEM((2, ROWS, FOLD), BF16),
            pltpu.VMEM((2, MX, 2 * DEEP, C * C), F32),
            pltpu.VMEM((2, MX, 2 * DEEP, HALF), F32),
            pltpu.VMEM(spectrum, BF16),
            pltpu.VMEM(spectrum, BF16),
            pltpu.VMEM((MX, 2 * DEEP, HALF), F32),
            pltpu.VMEM((2, GROUPS, mine, 2 * DEEP, HALF), BF16),
            pltpu.VMEM((2, GROUPS, mine, 2 * DEEP, HALF), BF16),
            pltpu.SemaphoreType.DMA((4, 2)),
            pltpu.SemaphoreType.DMA((STACKS,)),
            pltpu.SemaphoreType.DMA((8,)),
            pltpu.SemaphoreType.DMA((4, 2, 2)),
            pltpu.SemaphoreType.DMA((4, 2, 2)),
            pltpu.SemaphoreType.DMA((4, 2, 2)),
            pltpu.SemaphoreType.DMA((2, 2)),
            pltpu.SemaphoreType.DMA((2, 2)),
            pltpu.SemaphoreType.DMA((2, 2)),
            pltpu.SemaphoreType.REGULAR,
        ],
        compiler_params=pltpu.CompilerParams(
            collective_id=0, has_side_effects=True, vmem_limit_bytes=48 * 2**20
        ),
        cost_estimate=pl.CostEstimate(
            flops=5 * 10**9, bytes_accessed=16 * 2**20, transcendentals=2**21
        ),
    )(
        *(
            pltpu.with_memory_space_constraint(operand, pltpu.HBM)
            for operand in (
                fields.reshape(ROWS, PLANE),
                cotangent.reshape(ROWS, PLANE),
                spectral_weight,
                *constants,
            )
        )
    )
    grad_fields, grad_weight = pl.pallas_call(
        last_kernel,
        out_shape=(
            jax.ShapeDtypeStruct((ROWS, PLANE), BF16),
            jax.ShapeDtypeStruct((mine, 2, MZ, C * C), F32),
        ),
        in_specs=[vmem] * 5,
        out_specs=(any_space, any_space),
        scratch_shapes=[
            pltpu.VMEM((HALF, PLANE), BF16),
            pltpu.SemaphoreType.DMA((STORES + C * C // HALF,)),
            pltpu.SemaphoreType.DMA((4, 2)),
        ],
        compiler_params=pltpu.CompilerParams(vmem_limit_bytes=6 * 2**20),
    )(*(pltpu.with_memory_space_constraint(result, pltpu.VMEM) for result in results))
    return grad_fields.reshape(1, XD, C, PLANE), grad_weight


def solution(mesh):
    placed = (
        P("dp", "pencil", None, None),
        P("dp", "pencil", None, None),
        P(None, None, "pencil", None),
    )
    return jax.shard_map(
        per_device,
        mesh=mesh,
        in_specs=placed,
        out_specs=(P("dp", "pencil", None, None), P("dp", None, "pencil", None)),
        check_vma=False,
    )
```
